128 devices in a mesh: dom: 16 (over y, x), grp: 8 (over z, core).
Axes of the slice: x: 4, y: 4, z: 4, core: 2. Of those that a mesh axis runs over, the one named last changes fastest.
Arguments:
- modal_state: float32 [5, 8, 8, 8, 32768], P(None, None, None, None, ('dom', 'grp')), may hold values from -3 to 3
- velocity: float32 [3, 32768], P(None, ('dom', 'grp')), may hold values from -0.5 to 1
- density: float32 [32768], P(('dom', 'grp')), may hold values from 0.5 to 2
- sound_speed: float32 [32768], P(('dom', 'grp')), may hold values from 0.7 to 1.4
- stretch_first: float32 [16], P('dom'), may hold values from 1 to 4
- stretch_second: float32 [8], P('grp'), may hold values from 1 to 4
- stretch_third: float32 [256], replicated, may hold values from 1 to 4
- orders: int32 [256], P(('dom', 'grp')), may hold values from 3 to 7, as said below
Outputs:
- advanced: float32 [5, 8, 8, 8, 32768], P(None, None, None, None, ('dom', 'grp'))
The draws below stay inside these ranges and needn't reach their ends.
Inputs may be any that keep to these rules, and one draw needn't show every extreme that they name: `orders`: each tile of 128 consecutive elements carries one order.
All inputs are finite; a program needn't handle non-finite values.
Results may differ from the reference program's by a relative error of at most 0.0001.
Values sent between devices are 32-bit elements; how exact they have to be, the bound alone decides.
No kernel may reach another device: no remote copies, remote signals or barrier semaphores. Data moves between devices by JAX's collectives and lax.ppermute only.
A program may use at most 64 MiB of HBM per device.

```python
import math
import jax
import jax.numpy as jnp
from jax import lax

MODES = 8
BX = 1
BY = 1
BZ = 256
TILE = 128
ELEMS = 32768
EX = 16
EY = 8
TILES = 256
TILES_DEV = 2
N_DOM = 16
N_GRP = 8


def draw_orders(key, part):
    key = jax.random.fold_in(key, 7)
    tile_index = jnp.arange(TILES)
    group_index = tile_index // TILES_DEV % N_GRP
    distance = jnp.abs(2 * group_index + 1 - N_GRP)
    top_order = MODES - 1 - distance // 2
    lowered = jax.random.randint(key, (TILES,), 0, 2)
    return jnp.maximum(3, top_order - lowered).astype(jnp.int32)


def shard_levels(rng, dims, pieces, low, high):
    factor_of, own = 1.0, jax.random.fold_in(rng, 6)
    for position, parts in pieces:
        draws = jnp.exp(jax.random.uniform(jax.random.fold_in(own, position), (parts,), jnp.float32, low / len(pieces), high / len(pieces)))
        factor_of = factor_of * jnp.repeat(draws, dims[position] // parts).reshape([-1 if axis == position else 1 for axis in range(len(dims))])
    return factor_of


def centred(own_key, shape, scale, limit, pieces=(), held_as=jnp.bfloat16):
    array = scale * jax.random.normal(own_key, shape, jnp.float32)
    if pieces:
        array = array * shard_levels(own_key, shape, pieces, -0.22, 0.18)
    return jnp.clip(array, -limit, limit).astype(held_as)


def setup_inputs(seed: int = 0) -> dict:
    key_list = jax.random.split(jax.random.key(seed), 9)
    modal_state = centred(key_list[0], (5, MODES, MODES, MODES, ELEMS), 0.5, 3.0, ((4, 128),), jnp.float32)
    velocity = jnp.clip(-0.5 + 1.5 * jax.random.uniform(key_list[1], (3, ELEMS), jnp.float32) ** shard_levels(key_list[1], (3, ELEMS), ((1, 128),), -0.2, 0.2), -0.5, 1.0)
    density = jnp.clip(jnp.exp(math.log(2.0) - 1.3862944 * jax.random.uniform(key_list[2], (ELEMS,), jnp.float32) ** shard_levels(key_list[2], (ELEMS,), ((0, 128),), -0.2, 0.2)), 0.5, 2.0)
    sound_speed = jnp.clip(jnp.exp(math.log(1.4) - 0.6931472 * jax.random.uniform(key_list[3], (ELEMS,), jnp.float32) ** shard_levels(key_list[3], (ELEMS,), ((0, 128),), -0.2, 0.2)), 0.7, 1.4)
    stretch_first = jnp.clip(jnp.exp(math.log(4.0) - 1.3862944 * jax.random.uniform(key_list[4], (EX,), jnp.float32) ** shard_levels(key_list[4], (EX,), ((0, 16),), -0.2, 0.2)), 1.0, 4.0)
    stretch_second = jnp.clip(jnp.exp(math.log(4.0) - 1.3862944 * jax.random.uniform(key_list[5], (EY,), jnp.float32) ** shard_levels(key_list[5], (EY,), ((0, 8),), -0.2, 0.2)), 1.0, 4.0)
    stretch_third = jnp.clip(jnp.exp(jax.random.uniform(key_list[6], (BZ,), jnp.float32, math.log(1.0), math.log(4.0))), 1.0, 4.0)
    orders = draw_orders(jax.random.fold_in(key_list[8], 71), 0)
    return {"modal_state": modal_state, "velocity": velocity, "density": density, "sound_speed": sound_speed, "stretch_first": stretch_first, "stretch_second": stretch_second, "stretch_third": stretch_third, "orders": orders}


HALF_WAVE = 1.25
TIME_STEP = 0.01
SECTION_A2 = -0.4178904745
SECTION_B1 = 0.1496590219993
SECTION_B2 = 0.3792103129999
EINSUM_FORMS = ("mj,fjabe->fmabe", "mj,fajbe->fambe", "mj,fabje->fabme")


def stiffness(mode_count):
    row_index = jnp.arange(mode_count)[:, None]
    col_index = jnp.arange(mode_count)[None, :]
    nonzero = (col_index < row_index) & ((row_index + col_index) % 2 == 1)
    return jnp.where(nonzero, 2.0 * row_index + 1.0, 0.0).astype(jnp.float32)


def apply_flux(values, direction, velocity, density, sound_speed):
    flow_speed = velocity[direction]
    normal_part = values[1 + direction]
    mass_row = flow_speed * values[0] + density * normal_part
    moments = []
    for component in range(3):
        moment_term = flow_speed * values[1 + component]
        if component == direction:
            moment_term = moment_term + values[4] / density
        moments.append(moment_term)
    pressure_row = flow_speed * values[4] + density * sound_speed * sound_speed * normal_part
    return jnp.stack([mass_row] + moments + [pressure_row])


def along_modes(vector, direction):
    shape = [1, 1, 1, 1, 1]
    shape[1 + direction] = MODES
    return vector.reshape(shape)


def to_grid(values):
    leading = values.shape[:-1]
    depth = len(leading)
    blocks = values.reshape(leading + (N_DOM, N_GRP, BX, BY, BZ))
    blocks = jnp.moveaxis(blocks, depth + 2, depth + 1)
    return blocks.reshape(leading + (N_DOM * BX, N_GRP * BY, BZ))


def from_grid(grid_array):
    leading = grid_array.shape[:-3]
    depth = len(leading)
    blocks = grid_array.reshape(leading + (N_DOM, BX, N_GRP, BY, BZ))
    blocks = jnp.moveaxis(blocks, depth + 1, depth + 2)
    return blocks.reshape(leading + (ELEMS,))


def from_above(grid_array, mode_axis):
    remaining = lax.slice_in_dim(grid_array, 1, grid_array.shape[mode_axis], axis=mode_axis)
    boundary = jnp.zeros_like(lax.slice_in_dim(grid_array, 0, 1, axis=mode_axis))
    return jnp.concatenate([remaining, boundary], axis=mode_axis)


def from_below(grid_array, mode_axis):
    remaining = lax.slice_in_dim(grid_array, 0, grid_array.shape[mode_axis] - 1, axis=mode_axis)
    boundary = jnp.zeros_like(lax.slice_in_dim(grid_array, 0, 1, axis=mode_axis))
    return jnp.concatenate([boundary, remaining], axis=mode_axis)


def spatial_operator(field, mode_mask, velocity, density, sound_speed, metric):
    table = stiffness(MODES)
    alternating = (1 - 2 * (jnp.arange(MODES) % 2)).astype(jnp.float32)
    half_odd = (jnp.arange(MODES) + 0.5).astype(jnp.float32)
    summed = jnp.zeros_like(field)
    for direction in range(3):
        derivative = jnp.einsum(EINSUM_FORMS[direction], table, field, precision=lax.Precision.HIGHEST)
        volume = apply_flux(derivative, direction, velocity, density, sound_speed)
        upper_trace = jnp.sum(field, axis=1 + direction)
        lower_trace = jnp.sum(field * along_modes(alternating, direction), axis=1 + direction)
        own_upper = 0.5 * apply_flux(upper_trace, direction, velocity, density, sound_speed) + HALF_WAVE * upper_trace
        own_lower = -0.5 * apply_flux(lower_trace, direction, velocity, density, sound_speed) + HALF_WAVE * lower_trace
        lower_grid = to_grid(own_lower)
        upper_grid = to_grid(own_upper)
        if direction == 2:
            next_lower = jnp.roll(lower_grid, -1, axis=5)
            prior_upper = jnp.roll(upper_grid, 1, axis=5)
        else:
            next_lower = from_above(lower_grid, 3 + direction)
            prior_upper = from_below(upper_grid, 3 + direction)
        face_upper = own_upper - from_grid(next_lower)
        face_lower = own_lower - from_grid(prior_upper)
        lifted = along_modes(half_odd, direction) * (jnp.expand_dims(face_upper, 1 + direction) + along_modes(alternating, direction) * jnp.expand_dims(face_lower, 1 + direction))
        summed = summed + metric[direction] * (volume - lifted)
    return mode_mask * summed


def reference(modal_state, velocity, density, sound_speed, stretch_first, stretch_second, stretch_third, orders):
    grid_shape = (EX, EY, BZ)
    metric = jnp.stack([
        from_grid(jnp.broadcast_to(stretch_first[:, None, None], grid_shape)),
        from_grid(jnp.broadcast_to(stretch_second[None, :, None], grid_shape)),
        from_grid(jnp.broadcast_to(stretch_third[None, None, :], grid_shape)),
    ])
    element_order = jnp.repeat(orders, TILE)
    alive_modes = (jnp.arange(MODES)[:, None] <= element_order[None, :]).astype(jnp.float32)
    mode_mask = alive_modes[:, None, None, :] * alive_modes[None, :, None, :] * alive_modes[None, None, :, :]
    first_state = mode_mask * modal_state
    first_rate = TIME_STEP * spatial_operator(first_state, mode_mask, velocity, density, sound_speed, metric)
    second_state = first_state + SECTION_B1 * first_rate
    second_rate = SECTION_A2 * first_rate + TIME_STEP * spatial_operator(second_state, mode_mask, velocity, density, sound_speed, metric)
    return second_state + SECTION_B2 * second_rate
```

```python
import functools

import jax
import jax.numpy as jnp
from jax import lax
from jax.experimental import pallas as pl
from jax.experimental.pallas import tpu as pltpu
from jax.sharding import PartitionSpec as P

HALF_WAVE = 1.25
TIME_STEP = 0.01
SECTION_A2 = -0.4178904745
SECTION_B1 = 0.1496590219993
SECTION_B2 = 0.3792103129999
MODES = 8
FIELDS = 5
LANES = 128
TILES = 2
FACE = (TILES, FIELDS, MODES * MODES, LANES)
BULK = (TILES, FIELDS, MODES, MODES * MODES, LANES)
F32 = jnp.float32
VMEM_LIMIT = 24 * 1024 * 1024


def rows(m):
    if isinstance(m, int):
        return pl.ds(m * MODES, MODES)
    return pl.ds(pl.multiple_of(m * MODES, MODES), MODES)


def strided(m):
    return pl.ds(m, MODES, stride=MODES)


def flux(q, d, u, rho, inv, stiff):
    n = q[1 + d]
    out = [u * q[0] + rho * n, u * q[1], u * q[2], u * q[3], u * q[4] + stiff * n]
    out[1 + d] = out[1 + d] + inv * q[4]
    return out


def wide(ref, row, t):
    return jnp.broadcast_to(ref[row : row + 1, t * LANES : (t + 1) * LANES], (MODES, LANES))


def medium(vel, den, snd, t):
    rho = wide(den, 0, t)
    c = wide(snd, 0, t)
    return [wide(vel, k, t) for k in range(3)], rho, 1.0 / rho, rho * c * c


def levels(order):
    third = lax.broadcasted_iota(jnp.int32, (MODES, LANES), 0)
    return [jnp.where(jnp.maximum(third, k) <= order, 1.0, 0.0).astype(F32) for k in range(MODES)]


def place():
    out = []
    for axis in ("dom", "grp"):
        i = lax.axis_index(axis)
        n = lax.axis_size(axis)
        sign = (1 - 2 * lax.rem(i, 2)).astype(F32)
        has = jnp.logical_and(i > 0, i < n - 1)
        out.append((sign, has))
    return out


def write_faces(d, sign, coef, even_of, odd_of, slots, t):
    us, rho, inv, stiff = coef
    half = 0.5 * sign
    u = half * us[d]
    near, far = HALF_WAVE + u, HALF_WAVE - u
    rho, inv, stiff = half * rho, half * inv, half * stiff
    for m in range(MODES):
        even, odd = even_of(m), odd_of(m)
        odd = [sign * a for a in odd]
        one = flux([a + b for a, b in zip(even, odd)], d, near, rho, inv, stiff)
        two = flux([a - b for a, b in zip(even, odd)], d, far, -rho, -inv, -stiff)
        for f in range(FIELDS):
            slots[0][t, f, rows(m), :] = one[f]
            slots[1][t, f, rows(m), :] = two[f]


def halo_pair(slots, sign, has, t, f, m, scale):
    near = slots[0][t, f, rows(m), :]
    far = jnp.where(has, slots[1][t, f, rows(m), :], 0.0)
    return scale * (near + far), (scale * sign) * (near - far)


def first_faces(orders, vel, den, snd, modal, q0, x_even, x_odd, y_even, y_odd, sums, sems):
    copies = {}
    for t in range(TILES):
        for f in range(FIELDS):
            copies[t, f] = pltpu.make_async_copy(
                modal.at[f, :, :, pl.ds(t * LANES, LANES)], q0.at[t, f], sems.at[t, f]
            )
            copies[t, f].start()
    (sign_x, _), (sign_y, _) = place()
    for t in range(TILES):
        mask = levels(orders[t])
        for f in range(FIELDS):
            copies[t, f].wait()
            e0 = [None] * MODES
            o0 = [None] * MODES
            for a in range(MODES):
                e1 = o1 = None
                for b in range(MODES):
                    q = mask[max(a, b)] * q0[t, f, a, rows(b), :]
                    q0[t, f, a, rows(b), :] = q
                    if a % 2 == 0:
                        e0[b] = q if e0[b] is None else e0[b] + q
                    else:
                        o0[b] = q if o0[b] is None else o0[b] + q
                    if b % 2 == 0:
                        e1 = q if e1 is None else e1 + q
                    else:
                        o1 = q if o1 is None else o1 + q
                sums[2, f, rows(a), :] = e1
                sums[3, f, rows(a), :] = o1
            for b in range(MODES):
                sums[0, f, rows(b), :] = e0[b]
                sums[1, f, rows(b), :] = o0[b]
        coef = medium(vel, den, snd, t)
        for d, sign, slots in ((0, sign_x, (x_even, x_odd)), (1, sign_y, (y_even, y_odd))):
            write_faces(
                d,
                sign,
                coef,
                lambda m: [sums[2 * d, f, rows(m), :] for f in range(FIELDS)],
                lambda m: [sums[2 * d + 1, f, rows(m), :] for f in range(FIELDS)],
                slots,
                t,
            )


def scaled(coef, d, s):
    us, rho, inv, stiff = coef
    return s * us[d], s * rho, s * inv, s * stiff


def bases(d, even, odd, us, k):
    a_odd = flux(odd, d, *us)
    a_even = flux(even, d, *us)
    return (
        [-0.5 * (x + k * e) for x, e in zip(a_odd, even)],
        [-0.5 * (x + k * o) for x, o in zip(a_even, odd)],
    )


def parity_sums(load):
    even, odd = load(0), load(1)
    for m in range(2, MODES, 2):
        even = [a + b for a, b in zip(even, load(m))]
        odd = [a + b for a, b in zip(odd, load(m + 1))]
    return even, odd


def sweep(d, load, even, odd, us, emit):
    run = [even, odd]
    for m in range(MODES):
        here = run[m % 2]
        emit(m, [(2.0 * m + 1.0) * a for a in here] if m else here)
        if m < MODES - 1:
            w = flux(load(m), d, *us)
            run[1 - m % 2] = [a + b for a, b in zip(run[1 - m % 2], w)]


def third_direction(q, acc, coefs, g2, h):
    lane = lax.broadcasted_iota(jnp.int32, (MODES, LANES), 1)
    first, last = lane == 0, lane == LANES - 1

    def line(a, carry):
        def loader(t):
            return lambda m: [q[t, f, a, strided(m), :] for f in range(FIELDS)]

        own, up, down = [], [], []
        for t in range(TILES):
            even, odd = parity_sums(loader(t))
            own.append((even, odd))
            us, rho, inv, stiff = coefs[t]
            u = 0.5 * us[2]
            rho, inv, stiff = 0.5 * rho, 0.5 * inv, 0.5 * stiff
            upper = flux([x + y for x, y in zip(even, odd)], 2, HALF_WAVE + u, rho, inv, stiff)
            lower = flux([x - y for x, y in zip(even, odd)], 2, HALF_WAVE - u, -rho, -inv, -stiff)
            up.append([pltpu.roll(x, 1, 1) for x in upper])
            down.append([pltpu.roll(x, LANES - 1, 1) for x in lower])
        for t in range(TILES):
            s = h * g2[t]
            half = 0.5 * s
            us = scaled(coefs[t], 2, s)
            base_e, base_o = bases(2, *own[t], us, 2.0 * HALF_WAVE * s)
            for f in range(FIELDS):
                prior = jnp.where(first, up[1 - t][f], up[t][f])
                after = jnp.where(last, down[1 - t][f], down[t][f])
                base_e[f] = base_e[f] + half * (after + prior)
                base_o[f] = base_o[f] + half * (after - prior)

            def emit(m, terms):
                for f in range(FIELDS):
                    acc[t, f, a, strided(m), :] = terms[f]

            sweep(2, loader(t), base_e, base_o, us, emit)
        return carry

    lax.fori_loop(0, MODES, line, 0)


def second_direction(q, acc, coefs, g1, h):
    s = h * g1
    for t in range(TILES):
        us = scaled(coefs[t], 1, s)

        def line(a, carry):
            def load(m):
                return [q[t, f, a, rows(m), :] for f in range(FIELDS)]

            even, odd = parity_sums(load)
            base_e, base_o = bases(1, even, odd, us, 2.0 * HALF_WAVE * s)

            def emit(m, terms):
                for f in range(FIELDS):
                    acc[t, f, a, rows(m), :] = acc[t, f, a, rows(m), :] + terms[f]

            sweep(1, load, base_e, base_o, us, emit)
            return carry

        lax.fori_loop(0, MODES, line, 0)


def first_direction(q, acc, coefs, g0, h, finish):
    s = h * g0
    for t in range(TILES):
        us = scaled(coefs[t], 0, s)

        def line(b, carry):
            def load(m):
                return [q[t, f, m, rows(b), :] for f in range(FIELDS)]

            even, odd = parity_sums(load)
            base_e, base_o = bases(0, even, odd, us, 2.0 * HALF_WAVE * s)

            def emit(m, terms):
                finish(t, m, b, [acc[t, f, m, rows(b), :] + terms[f] for f in range(FIELDS)])

            sweep(0, load, base_e, base_o, us, emit)
            return carry

        lax.fori_loop(0, MODES, line, 0)


def store_levels(orders, mask_ref):
    for t in range(TILES):
        for k, level in enumerate(levels(orders[t])):
            mask_ref[t, k] = level


def local_rate(orders, g0, g1, vel, den, snd, g2_ref, q0, r1, traces, acc, mask_ref):
    coefs = [medium(vel, den, snd, t) for t in range(TILES)]
    g2 = [wide(g2_ref, 0, t) for t in range(TILES)]
    store_levels(orders, mask_ref)
    traces[...] = jnp.zeros(traces.shape, F32)
    third_direction(q0, acc, coefs, g2, TIME_STEP)
    second_direction(q0, acc, coefs, g1[0], TIME_STEP)

    def finish(t, a, b, totals):
        level = mask_ref[t, jnp.maximum(a, b)]
        slot = 2 + lax.rem(b, 2)
        for f in range(FIELDS):
            rate = level * totals[f]
            r1[t, f, a, rows(b), :] = rate
            q = q0[t, f, a, rows(b), :] + SECTION_B1 * rate
            traces[a % 2, t, f, rows(b), :] = traces[a % 2, t, f, rows(b), :] + q
            traces[slot, t, f, rows(a), :] = traces[slot, t, f, rows(a), :] + q

    first_direction(q0, acc, coefs, g0[0], TIME_STEP, finish)


def second_faces(
    orders, g0, g1, vel, den, snd, traces, xe, xo, ye, yo, x_even, x_odd, y_even, y_odd, face
):
    (sign_x, has_x), (sign_y, has_y) = place()
    for t in range(TILES):
        order = orders[t]
        mask = levels(order)
        weights = [
            sum(jnp.where(m <= order, m + 0.5, 0.0) for m in range(parity, MODES, 2)) for parity in range(2)
        ]
        scale = (SECTION_B1 * TIME_STEP * g0[0], SECTION_B1 * TIME_STEP * g1[0])
        for f in range(FIELDS):
            pairs = []
            across = []
            for d, slots, sign, has in ((0, (xe, xo), sign_x, has_x), (1, (ye, yo), sign_y, has_y)):
                pair = [halo_pair(slots, sign, has, t, f, m, scale[d]) for m in range(MODES)]
                pairs.append(pair)
                across.append(
                    [
                        [sum(mask[m] * pair[m][kind] for m in range(parity, MODES, 2)) for parity in range(2)]
                        for kind in range(2)
                    ]
                )
            for d in range(2):
                for m in range(MODES):
                    for parity in range(2):
                        add = weights[parity] * pairs[d][m][parity] + (m + 0.5) * across[1 - d][m % 2][parity]
                        face[2 * d + parity, f, rows(m), :] = (
                            traces[2 * d + parity, t, f, rows(m), :] + mask[m] * add
                        )
        coef = medium(vel, den, snd, t)
        for d, sign, slots in ((0, sign_x, (x_even, x_odd)), (1, sign_y, (y_even, y_odd))):
            write_faces(
                d,
                sign,
                coef,
                lambda m: [face[2 * d, f, rows(m), :] for f in range(FIELDS)],
                lambda m: [face[2 * d + 1, f, rows(m), :] for f in range(FIELDS)],
                slots,
                t,
            )


def store_halos(halo, xe, xo, ye, yo, scale_x, scale_y):
    (sign_x, has_x), (sign_y, has_y) = place()
    for d, slots, sign, has, scale in ((0, (xe, xo), sign_x, has_x, scale_x), (1, (ye, yo), sign_y, has_y, scale_y)):
        for t in range(TILES):

            def one(f, carry):
                for m in range(MODES):
                    plus, minus = halo_pair(slots, sign, has, t, f, m, scale)
                    halo[d, 0, t, f, rows(m), :] = plus
                    halo[d, 1, t, f, rows(m), :] = minus
                return carry

            lax.fori_loop(0, FIELDS, one, 0)


def halo_term(halo, t, f, a, b, weight, kind):
    return (a + 0.5) * halo[0, a % 2, t, f, rows(b), :] + weight * halo[1, kind, t, f, rows(a), :]


def second_local(
    orders, g0, g1, vel, den, snd, g2_ref, q0, r1, xe, xo, ye, yo, part, q1, acc, halo, mask_ref
):
    coefs = [medium(vel, den, snd, t) for t in range(TILES)]
    g2 = [wide(g2_ref, 0, t) for t in range(TILES)]
    store_levels(orders, mask_ref)
    store_halos(halo, xe, xo, ye, yo, TIME_STEP * g0[0], TIME_STEP * g1[0])
    for t in range(TILES):

        def column(b, carry):
            weight = b.astype(F32) + 0.5
            kind = lax.rem(b, 2)
            for a in range(MODES):
                level = mask_ref[t, jnp.maximum(a, b)]
                for f in range(FIELDS):
                    rate = r1[t, f, a, rows(b), :] + level * halo_term(halo, t, f, a, b, weight, kind)
                    q = q0[t, f, a, rows(b), :] + SECTION_B1 * rate
                    q1[t, f, a, rows(b), :] = q
                    part[t, f, a, rows(b), :] = q + (SECTION_B2 * SECTION_A2) * rate
            return carry

        lax.fori_loop(0, MODES, column, 0)
    third_direction(q1, acc, coefs, g2, SECTION_B2 * TIME_STEP)
    second_direction(q1, acc, coefs, g1[0], SECTION_B2 * TIME_STEP)

    def finish(t, a, b, totals):
        level = mask_ref[t, jnp.maximum(a, b)]
        for f in range(FIELDS):
            part[t, f, a, rows(b), :] = part[t, f, a, rows(b), :] + level * totals[f]

    first_direction(q1, acc, coefs, g0[0], SECTION_B2 * TIME_STEP, finish)


def last_add(orders, g0, g1, part, xe, xo, ye, yo, out, done, halo, sems):
    s = SECTION_B2 * TIME_STEP
    store_halos(halo, xe, xo, ye, yo, s * g0[0], s * g1[0])
    copies = []
    for t in range(TILES):
        mask = levels(orders[t])
        for f in range(FIELDS):
            for a in range(MODES):
                for b in range(MODES):
                    term = halo_term(halo, t, f, a, b, b + 0.5, b % 2)
                    done[t, f, a, rows(b), :] = part[t, f, a, rows(b), :] + mask[max(a, b)] * term
            copy = pltpu.make_async_copy(done.at[t, f], out.at[f, :, :, pl.ds(t * LANES, LANES)], sems.at[t, f])
            copy.start()
            copies.append(copy)
    for copy in copies:
        copy.wait()


SCALAR = pl.BlockSpec(memory_space=pltpu.SMEM)
LOCAL = pl.BlockSpec(memory_space=pltpu.VMEM)
ANYWHERE = pl.BlockSpec(memory_space=pl.ANY)


def call(body, operands, specs, outs, out_specs, scratch, cost):
    return pl.pallas_call(
        body,
        out_shape=outs,
        in_specs=specs,
        out_specs=out_specs,
        scratch_shapes=scratch,
        compiler_params=pltpu.CompilerParams(vmem_limit_bytes=VMEM_LIMIT),
        cost_estimate=pl.CostEstimate(flops=cost, bytes_accessed=2_600_000, transcendentals=0),
        name=body.__name__,
    )(*operands)


def exchange(dom_perms, grp_perms, faces):
    x_even, x_odd, y_even, y_odd = faces
    both = ("dom", "grp")
    return (
        lax.ppermute(x_even, "dom", dom_perms[0]),
        lax.ppermute(x_odd, both, dom_perms[1]),
        lax.ppermute(y_even, "grp", grp_perms[0]),
        lax.ppermute(y_odd, "grp", grp_perms[1]),
    )


def pair_swaps(n_dom, n_grp):
    even = lambda n: [(i, i ^ 1) for i in range(n)]
    other = lambda i: ((i - 1) ^ 1) + 1
    dom_odd = []
    for i in range(n_dom):
        for j in range(n_grp):
            if 0 < i < n_dom - 1:
                target = other(i) * n_grp + j
            else:
                target = i * n_grp + (j ^ 1)
            dom_odd.append((i * n_grp + j, target))
    grp_odd = [(j, other(j) if 0 < j < n_grp - 1 else n_grp - 1 - j) for j in range(n_grp)]
    return (even(n_dom), dom_odd), (even(n_grp), grp_odd)


def per_device(n_dom, n_grp, modal, vel, den, snd, g0, g1, g2, orders):
    dom_perms, grp_perms = pair_swaps(n_dom, n_grp)
    swap = functools.partial(exchange, dom_perms, grp_perms)
    shape = modal.shape
    modal = modal.reshape(FIELDS, MODES, MODES * MODES, TILES * LANES)
    den, snd, g2 = (x.reshape(1, TILES * LANES) for x in (den, snd, g2))
    face = jax.ShapeDtypeStruct(FACE, F32)
    bulk = jax.ShapeDtypeStruct(BULK, F32)
    sems = pltpu.SemaphoreType.DMA((TILES, FIELDS))
    plane = (FIELDS, MODES * MODES, LANES)
    q0, *faces = call(
        first_faces,
        (orders, vel, den, snd, modal),
        [SCALAR, LOCAL, LOCAL, LOCAL, ANYWHERE],
        (bulk,) + (face,) * 4,
        (LOCAL,) * 5,
        [pltpu.VMEM((4,) + plane, F32), sems],
        2_000_000,
    )
    halos = swap(faces)
    masks = pltpu.VMEM((TILES, MODES, MODES, LANES), F32)
    r1, traces = call(
        local_rate,
        (orders, g0, g1, vel, den, snd, g2, q0),
        [SCALAR] * 3 + [LOCAL] * 5,
        (bulk, jax.ShapeDtypeStruct((4,) + FACE, F32)),
        (LOCAL,) * 2,
        [pltpu.VMEM(BULK, F32), masks],
        16_000_000,
    )
    faces = call(
        second_faces,
        (orders, g0, g1, vel, den, snd, traces, *halos),
        [SCALAR] * 3 + [LOCAL] * 8,
        (face,) * 4,
        (LOCAL,) * 4,
        [pltpu.VMEM((4,) + plane, F32)],
        2_000_000,
    )
    last = swap(faces)
    halo = pltpu.VMEM((2, 2) + FACE, F32)
    part = call(
        second_local,
        (orders, g0, g1, vel, den, snd, g2, q0, r1, *halos),
        [SCALAR] * 3 + [LOCAL] * 10,
        bulk,
        LOCAL,
        [pltpu.VMEM(BULK, F32), pltpu.VMEM(BULK, F32), halo, masks],
        20_000_000,
    )
    out = call(
        last_add,
        (orders, g0, g1, part, *last),
        [SCALAR] * 3 + [LOCAL] * 5,
        jax.ShapeDtypeStruct(modal.shape, F32),
        ANYWHERE,
        [pltpu.VMEM(BULK, F32), halo, sems],
        4_000_000,
    )
    return out.reshape(shape)


def solution(mesh):
    placed = (
        P(None, None, None, None, ("dom", "grp")),
        P(None, ("dom", "grp")),
        P(("dom", "grp")),
        P(("dom", "grp")),
        P("dom"),
        P("grp"),
        P(),
        P(("dom", "grp")),
    )
    return jax.shard_map(
        functools.partial(per_device, mesh.shape["dom"], mesh.shape["grp"]),
        mesh=mesh,
        in_specs=placed,
        out_specs=P(None, None, None, None, ("dom", "grp")),
        check_vma=False,
    )
```

```python
import functools

import jax
import jax.numpy as jnp
from jax import lax
from jax.experimental import pallas as pl
from jax.experimental.pallas import tpu as pltpu
from jax.sharding import PartitionSpec as P

HALF_WAVE = 1.25
TIME_STEP = 0.01
SECTION_A2 = -0.4178904745
SECTION_B1 = 0.1496590219993
SECTION_B2 = 0.3792103129999
MODES = 8
FIELDS = 5
LANES = 128
TILES = 2
FACE = (TILES, FIELDS, MODES * MODES, LANES)
BULK = (TILES, FIELDS, MODES, MODES * MODES, LANES)
F32 = jnp.float32
VMEM_LIMIT = 24 * 1024 * 1024


def rows(m):
    if isinstance(m, int):
        return pl.ds(m * MODES, MODES)
    return pl.ds(pl.multiple_of(m * MODES, MODES), MODES)


def strided(m):
    return pl.ds(m, MODES, stride=MODES)


def flux(q, d, u, rho, inv, stiff):
    n = q[1 + d]
    out = [u * q[0] + rho * n, u * q[1], u * q[2], u * q[3], u * q[4] + stiff * n]
    out[1 + d] = out[1 + d] + inv * q[4]
    return out


FLOW, RHO, INVERSE, STIFF, THIRD, LEVEL, WEIGHT = 0, 3, 4, 5, 6, 7, 15
COEFS = (TILES, 17, MODES, LANES)


def spread(ref, t, row=0):
    lanes = pl.ds(t * LANES, LANES)
    part = ref[lanes].reshape(1, -1) if len(ref.shape) == 1 else ref[pl.ds(row, 1), lanes]
    return jnp.broadcast_to(part, (MODES, LANES))


def store_coefs(coefs, vel, den, snd, g2, orders):
    third = lax.broadcasted_iota(jnp.int32, (MODES, LANES), 0)
    for t in range(TILES):
        for k in range(3):
            coefs[t, FLOW + k] = spread(vel, t, k)
        rho, c = spread(den, t), spread(snd, t)
        coefs[t, RHO] = rho
        coefs[t, INVERSE] = 1.0 / rho
        coefs[t, STIFF] = rho * c * c
        coefs[t, THIRD] = spread(g2, t)
        order = jnp.broadcast_to(orders[pl.ds(t, 1)].reshape(1, 1), (MODES, LANES))
        for k in range(MODES):
            coefs[t, LEVEL + k] = jnp.where(jnp.maximum(third, k) <= order, 1.0, 0.0).astype(F32)
        for parity in range(2):
            coefs[t, WEIGHT + parity] = sum(
                jnp.where(order >= m, m + 0.5, 0.0).astype(F32) for m in range(parity, MODES, 2)
            )


def medium(coefs, t):
    return [coefs[t, FLOW + k] for k in range(3)], coefs[t, RHO], coefs[t, INVERSE], coefs[t, STIFF]


def place():
    out = []
    for axis in ("dom", "grp"):
        i = lax.axis_index(axis)
        n = lax.axis_size(axis)
        sign = (1 - 2 * lax.rem(i, 2)).astype(F32)
        has = jnp.logical_and(i > 0, i < n - 1)
        out.append((sign, has))
    return out


def write_faces(d, sign, coef, even_of, odd_of, slots, t):
    us, rho, inv, stiff = coef
    half = 0.5 * sign
    u = half * us[d]
    near, far = HALF_WAVE + u, HALF_WAVE - u
    rho, inv, stiff = half * rho, half * inv, half * stiff
    for m in range(MODES):
        even, odd = even_of(m), odd_of(m)
        odd = [sign * a for a in odd]
        one = flux([a + b for a, b in zip(even, odd)], d, near, rho, inv, stiff)
        two = flux([a - b for a, b in zip(even, odd)], d, far, -rho, -inv, -stiff)
        for f in range(FIELDS):
            slots[0][t, f, rows(m), :] = one[f]
            slots[1][t, f, rows(m), :] = two[f]


def halo_pair(slots, sign, has, t, f, m, scale):
    near = slots[0][t, f, rows(m), :]
    far = jnp.where(has, slots[1][t, f, rows(m), :], 0.0)
    return scale * (near + far), (scale * sign) * (near - far)


def first_faces(*refs):
    small, (modal, q0, coefs, x_even, x_odd, y_even, y_odd), (sums, sems, *held, small_sems) = refs[:5], refs[5:12], refs[12:]
    loads = [pltpu.make_async_copy(a, b, small_sems.at[i]) for i, (a, b) in enumerate(zip(small, held))]
    for load in loads:
        load.start()
    copies = {}
    for t in range(TILES):
        for f in range(FIELDS):
            copies[t, f] = pltpu.make_async_copy(
                modal.at[f, :, :, pl.ds(t * LANES, LANES)], q0.at[t, f], sems.at[t, f]
            )
            copies[t, f].start()
    (sign_x, _), (sign_y, _) = place()
    for load in loads:
        load.wait()
    store_coefs(coefs, *held)
    for t in range(TILES):
        for f in range(FIELDS):
            copies[t, f].wait()
            e0 = [None] * MODES
            o0 = [None] * MODES
            for a in range(MODES):
                e1 = o1 = None
                for b in range(MODES):
                    q = coefs[t, LEVEL + max(a, b)] * q0[t, f, a, rows(b), :]
                    q0[t, f, a, rows(b), :] = q
                    if a % 2 == 0:
                        e0[b] = q if e0[b] is None else e0[b] + q
                    else:
                        o0[b] = q if o0[b] is None else o0[b] + q
                    if b % 2 == 0:
                        e1 = q if e1 is None else e1 + q
                    else:
                        o1 = q if o1 is None else o1 + q
                sums[2, f, rows(a), :] = e1
                sums[3, f, rows(a), :] = o1
            for b in range(MODES):
                sums[0, f, rows(b), :] = e0[b]
                sums[1, f, rows(b), :] = o0[b]
        coef = medium(coefs, t)
        for d, sign, slots in ((0, sign_x, (x_even, x_odd)), (1, sign_y, (y_even, y_odd))):
            write_faces(
                d,
                sign,
                coef,
                lambda m: [sums[2 * d, f, rows(m), :] for f in range(FIELDS)],
                lambda m: [sums[2 * d + 1, f, rows(m), :] for f in range(FIELDS)],
                slots,
                t,
            )


def scaled(coef, d, s):
    us, rho, inv, stiff = coef
    return s * us[d], s * rho, s * inv, s * stiff


def bases(d, even, odd, us, k):
    a_odd = flux(odd, d, *us)
    a_even = flux(even, d, *us)
    return (
        [-0.5 * (x + k * e) for x, e in zip(a_odd, even)],
        [-0.5 * (x + k * o) for x, o in zip(a_even, odd)],
    )


def parity_sums(load):
    even, odd = load(0), load(1)
    for m in range(2, MODES, 2):
        even = [a + b for a, b in zip(even, load(m))]
        odd = [a + b for a, b in zip(odd, load(m + 1))]
    return even, odd


def sweep(d, load, even, odd, us, emit):
    run = [even, odd]
    for m in range(MODES):
        here = run[m % 2]
        emit(m, [(2.0 * m + 1.0) * a for a in here] if m else here)
        if m < MODES - 1:
            w = flux(load(m), d, *us)
            run[1 - m % 2] = [a + b for a, b in zip(run[1 - m % 2], w)]


def third_direction(q, acc, coefs, metric, h):
    lane = lax.broadcasted_iota(jnp.int32, (MODES, LANES), 1)
    first, last = lane == 0, lane == LANES - 1

    def line(a, carry):
        def loader(t):
            return lambda m: [q[t, f, a, strided(m), :] for f in range(FIELDS)]

        own, up, down = [], [], []
        for t in range(TILES):
            even, odd = parity_sums(loader(t))
            own.append((even, odd))
            us, rho, inv, stiff = medium(coefs, t)
            u = 0.5 * us[2]
            rho, inv, stiff = 0.5 * rho, 0.5 * inv, 0.5 * stiff
            upper = flux([x + y for x, y in zip(even, odd)], 2, HALF_WAVE + u, rho, inv, stiff)
            lower = flux([x - y for x, y in zip(even, odd)], 2, HALF_WAVE - u, -rho, -inv, -stiff)
            up.append([pltpu.roll(x, 1, 1) for x in upper])
            down.append([pltpu.roll(x, LANES - 1, 1) for x in lower])
        for t in range(TILES):
            s = h * coefs[t, THIRD]
            half = 0.5 * s
            us = scaled(medium(coefs, t), 2, s)
            base_e, base_o = bases(2, *own[t], us, 2.0 * HALF_WAVE * s)
            for f in range(FIELDS):
                prior = jnp.where(first, up[1 - t][f], up[t][f])
                after = jnp.where(last, down[1 - t][f], down[t][f])
                base_e[f] = base_e[f] + half * (after + prior)
                base_o[f] = base_o[f] + half * (after - prior)

            def emit(m, terms):
                for f in range(FIELDS):
                    acc[t, f, a, strided(m), :] = terms[f]

            sweep(2, loader(t), base_e, base_o, us, emit)
        return carry

    lax.fori_loop(0, MODES, line, 0)


def second_direction(q, acc, coefs, metric, h):
    for t in range(TILES):
        s = h * metric[1]
        us = scaled(medium(coefs, t), 1, s)

        def line(a, carry):
            def load(m):
                return [q[t, f, a, rows(m), :] for f in range(FIELDS)]

            even, odd = parity_sums(load)
            base_e, base_o = bases(1, even, odd, us, 2.0 * HALF_WAVE * s)

            def emit(m, terms):
                for f in range(FIELDS):
                    acc[t, f, a, rows(m), :] = acc[t, f, a, rows(m), :] + terms[f]

            sweep(1, load, base_e, base_o, us, emit)
            return carry

        lax.fori_loop(0, MODES, line, 0)


def first_direction(q, acc, coefs, metric, h, finish):
    for t in range(TILES):
        s = h * metric[0]
        us = scaled(medium(coefs, t), 0, s)

        def line(b, carry):
            def load(m):
                return [q[t, f, m, rows(b), :] for f in range(FIELDS)]

            even, odd = parity_sums(load)
            base_e, base_o = bases(0, even, odd, us, 2.0 * HALF_WAVE * s)

            kept = {}

            def emit(m, terms):
                finish(t, b, m, [acc[t, f, m, rows(b), :] + terms[f] for f in range(FIELDS)], kept)

            sweep(0, load, base_e, base_o, us, emit)
            return carry

        lax.fori_loop(0, MODES, line, 0)


def local_rate(coefs, g0, g1, q0, r1, traces, acc):
    metric = g0[0], g1[0]
    traces[pl.ds(2, 2)] = jnp.zeros((2,) + FACE, F32)
    third_direction(q0, acc, coefs, metric, TIME_STEP)
    second_direction(q0, acc, coefs, metric, TIME_STEP)

    def finish(t, b, a, totals, kept):
        level = coefs[t, LEVEL + jnp.maximum(a, b)]
        slot = 2 + lax.rem(b, 2)
        for f in range(FIELDS):
            rate = level * totals[f]
            r1[t, f, a, rows(b), :] = rate
            q = q0[t, f, a, rows(b), :] + SECTION_B1 * rate
            kept[a % 2, f] = q if a < 2 else kept[a % 2, f] + q
            traces[slot, t, f, rows(a), :] = traces[slot, t, f, rows(a), :] + q
        if a == MODES - 1:
            for (parity, f), total in kept.items():
                traces[parity, t, f, rows(b), :] = total

    first_direction(q0, acc, coefs, metric, TIME_STEP, finish)


def second_faces(coefs, g0, g1, traces, xe, xo, ye, yo, x_even, x_odd, y_even, y_odd, face):
    metric = g0[0], g1[0]
    (sign_x, has_x), (sign_y, has_y) = place()
    for t in range(TILES):
        mask = [coefs[t, LEVEL + k] for k in range(MODES)]
        weights = [coefs[t, WEIGHT + parity] for parity in range(2)]
        scale = [SECTION_B1 * TIME_STEP * metric[d] for d in range(2)]
        for f in range(FIELDS):
            pairs = []
            across = []
            for d, slots, sign, has in ((0, (xe, xo), sign_x, has_x), (1, (ye, yo), sign_y, has_y)):
                pair = [halo_pair(slots, sign, has, t, f, m, scale[d]) for m in range(MODES)]
                pairs.append(pair)
                across.append(
                    [
                        [sum(mask[m] * pair[m][kind] for m in range(parity, MODES, 2)) for parity in range(2)]
                        for kind in range(2)
                    ]
                )
            for d in range(2):
                for m in range(MODES):
                    for parity in range(2):
                        add = weights[parity] * pairs[d][m][parity] + (m + 0.5) * across[1 - d][m % 2][parity]
                        face[2 * d + parity, f, rows(m), :] = (
                            traces[2 * d + parity, t, f, rows(m), :] + mask[m] * add
                        )
        coef = medium(coefs, t)
        for d, sign, slots in ((0, sign_x, (x_even, x_odd)), (1, sign_y, (y_even, y_odd))):
            write_faces(
                d,
                sign,
                coef,
                lambda m: [face[2 * d, f, rows(m), :] for f in range(FIELDS)],
                lambda m: [face[2 * d + 1, f, rows(m), :] for f in range(FIELDS)],
                slots,
                t,
            )


def store_halos(halo, xe, xo, ye, yo, metric, s):
    (sign_x, has_x), (sign_y, has_y) = place()
    for d, slots, sign, has in ((0, (xe, xo), sign_x, has_x), (1, (ye, yo), sign_y, has_y)):
        for t in range(TILES):
            scale = s * metric[d]

            def one(f, carry):
                for m in range(MODES):
                    plus, minus = halo_pair(slots, sign, has, t, f, m, scale)
                    halo[d, 0, t, f, rows(m), :] = plus
                    halo[d, 1, t, f, rows(m), :] = minus
                return carry

            lax.fori_loop(0, FIELDS, one, 0)


def halo_term(halo, t, f, a, b, weight, kind):
    return (a + 0.5) * halo[0, a % 2, t, f, rows(b), :] + weight * halo[1, kind, t, f, rows(a), :]


def second_local(coefs, g0, g1, q0, r1, xe, xo, ye, yo, part, q1, acc, halo):
    metric = g0[0], g1[0]
    store_halos(halo, xe, xo, ye, yo, metric, TIME_STEP)
    for t in range(TILES):

        def column(b, carry):
            weight = b.astype(F32) + 0.5
            kind = lax.rem(b, 2)
            for a in range(MODES):
                level = coefs[t, LEVEL + jnp.maximum(a, b)]
                for f in range(FIELDS):
                    rate = r1[t, f, a, rows(b), :] + level * halo_term(halo, t, f, a, b, weight, kind)
                    q = q0[t, f, a, rows(b), :] + SECTION_B1 * rate
                    q1[t, f, a, rows(b), :] = q
                    part[t, f, a, rows(b), :] = q + (SECTION_B2 * SECTION_A2) * rate
            return carry

        lax.fori_loop(0, MODES, column, 0)
    third_direction(q1, acc, coefs, metric, SECTION_B2 * TIME_STEP)
    second_direction(q1, acc, coefs, metric, SECTION_B2 * TIME_STEP)

    def finish(t, b, a, totals, kept):
        level = coefs[t, LEVEL + jnp.maximum(a, b)]
        for f in range(FIELDS):
            part[t, f, a, rows(b), :] = part[t, f, a, rows(b), :] + level * totals[f]

    first_direction(q1, acc, coefs, metric, SECTION_B2 * TIME_STEP, finish)


def last_add(coefs, g0, g1, part, xe, xo, ye, yo, out, done, halo, sems):
    metric = g0[0], g1[0]
    store_halos(halo, xe, xo, ye, yo, metric, SECTION_B2 * TIME_STEP)
    copies = []
    for t in range(TILES):
        mask = [coefs[t, LEVEL + k] for k in range(MODES)]
        for f in range(FIELDS):
            for a in range(MODES):
                for b in range(MODES):
                    term = halo_term(halo, t, f, a, b, b + 0.5, b % 2)
                    done[t, f, a, rows(b), :] = part[t, f, a, rows(b), :] + mask[max(a, b)] * term
            copy = pltpu.make_async_copy(done.at[t, f], out.at[f, :, :, pl.ds(t * LANES, LANES)], sems.at[t, f])
            copy.start()
            copies.append(copy)
    for copy in copies:
        copy.wait()


SCALAR = pl.BlockSpec(memory_space=pltpu.SMEM)
LOCAL = pl.BlockSpec(memory_space=pltpu.VMEM)
FAR = pl.BlockSpec(memory_space=pltpu.HBM)


def call(body, operands, specs, outs, out_specs, scratch, cost):
    return pl.pallas_call(
        body,
        out_shape=outs,
        in_specs=specs,
        out_specs=out_specs,
        scratch_shapes=scratch,
        compiler_params=pltpu.CompilerParams(vmem_limit_bytes=VMEM_LIMIT),
        cost_estimate=pl.CostEstimate(flops=cost, bytes_accessed=2_600_000, transcendentals=0),
        name=body.__name__,
    )(*operands)


def exchange(dom_perms, grp_perms, faces):
    x_even, x_odd, y_even, y_odd = faces
    both = ("dom", "grp")
    return (
        lax.ppermute(x_even, "dom", dom_perms[0]),
        lax.ppermute(x_odd, both, dom_perms[1]),
        lax.ppermute(y_even, "grp", grp_perms[0]),
        lax.ppermute(y_odd, "grp", grp_perms[1]),
    )


def pair_swaps(n_dom, n_grp):
    even = lambda n: [(i, i ^ 1) for i in range(n)]
    other = lambda i: ((i - 1) ^ 1) + 1
    dom_odd = []
    for i in range(n_dom):
        for j in range(n_grp):
            if 0 < i < n_dom - 1:
                target = other(i) * n_grp + j
            else:
                target = i * n_grp + (j ^ 1)
            dom_odd.append((i * n_grp + j, target))
    grp_odd = [(j, other(j) if 0 < j < n_grp - 1 else n_grp - 1 - j) for j in range(n_grp)]
    return (even(n_dom), dom_odd), (even(n_grp), grp_odd)


def per_device(n_dom, n_grp, modal, vel, den, snd, g0, g1, g2, orders):
    dom_perms, grp_perms = pair_swaps(n_dom, n_grp)
    swap = functools.partial(exchange, dom_perms, grp_perms)
    shape = modal.shape
    modal = modal.reshape(FIELDS, MODES, MODES * MODES, TILES * LANES)
    small = [vel, den, snd, g2, orders]
    face = jax.ShapeDtypeStruct(FACE, F32)
    bulk = jax.ShapeDtypeStruct(BULK, F32)
    sems = pltpu.SemaphoreType.DMA((TILES, FIELDS))
    plane = (FIELDS, MODES * MODES, LANES)
    q0, coefs, *faces = call(
        first_faces,
        tuple(pltpu.with_memory_space_constraint(x, pltpu.HBM) for x in (*small, modal)),
        [FAR] * 6,
        (bulk, jax.ShapeDtypeStruct(COEFS, F32)) + (face,) * 4,
        (LOCAL,) * 6,
        [pltpu.VMEM((4,) + plane, F32), sems]
        + [pltpu.VMEM(x.shape, x.dtype) for x in small]
        + [pltpu.SemaphoreType.DMA((len(small),))],
        2_000_000,
    )
    halos = swap(faces)
    r1, traces = call(
        local_rate,
        (coefs, g0, g1, q0),
        [LOCAL, SCALAR, SCALAR, LOCAL],
        (bulk, jax.ShapeDtypeStruct((4,) + FACE, F32)),
        (LOCAL,) * 2,
        [pltpu.VMEM(BULK, F32)],
        16_000_000,
    )
    faces = call(
        second_faces,
        (coefs, g0, g1, traces, *halos),
        [LOCAL, SCALAR, SCALAR] + [LOCAL] * 5,
        (face,) * 4,
        (LOCAL,) * 4,
        [pltpu.VMEM((4,) + plane, F32)],
        2_000_000,
    )
    last = swap(faces)
    halo = pltpu.VMEM((2, 2) + FACE, F32)
    part = call(
        second_local,
        (coefs, g0, g1, q0, r1, *halos),
        [LOCAL, SCALAR, SCALAR] + [LOCAL] * 6,
        bulk,
        LOCAL,
        [pltpu.VMEM(BULK, F32), pltpu.VMEM(BULK, F32), halo],
        20_000_000,
    )
    out = call(
        last_add,
        (coefs, g0, g1, part, *last),
        [LOCAL, SCALAR, SCALAR] + [LOCAL] * 5,
        jax.ShapeDtypeStruct(modal.shape, F32),
        FAR,
        [pltpu.VMEM(BULK, F32), halo, sems],
        4_000_000,
    )
    return out.reshape(shape)


def solution(mesh):
    placed = (
        P(None, None, None, None, ("dom", "grp")),
        P(None, ("dom", "grp")),
        P(("dom", "grp")),
        P(("dom", "grp")),
        P("dom"),
        P("grp"),
        P(),
        P(("dom", "grp")),
    )
    return jax.shard_map(
        functools.partial(per_device, mesh.shape["dom"], mesh.shape["grp"]),
        mesh=mesh,
        in_specs=placed,
        out_specs=P(None, None, None, None, ("dom", "grp")),
        check_vma=False,
    )
```

```python
import functools

import jax
import jax.numpy as jnp
from jax import lax
from jax.experimental import pallas as pl
from jax.experimental.pallas import tpu as pltpu
from jax.sharding import PartitionSpec as P

HALF_WAVE = 1.25
TIME_STEP = 0.01
SECTION_A2 = -0.4178904745
SECTION_B1 = 0.1496590219993
SECTION_B2 = 0.3792103129999
MODES = 8
FIELDS = 5
LANES = 128
TILES = 2
FACE = (TILES, FIELDS, MODES * MODES, LANES)
BULK = (TILES, FIELDS, MODES, MODES * MODES, LANES)
F32 = jnp.float32
VMEM_LIMIT = 24 * 1024 * 1024


def rows(m):
    if isinstance(m, int):
        return pl.ds(m * MODES, MODES)
    return pl.ds(pl.multiple_of(m * MODES, MODES), MODES)


def strided(m):
    return pl.ds(m, MODES, stride=MODES)


def flux(q, d, u, rho, inv, stiff):
    n = q[1 + d]
    out = [u * q[0] + rho * n, u * q[1], u * q[2], u * q[3], u * q[4] + stiff * n]
    out[1 + d] = out[1 + d] + inv * q[4]
    return out


FLOW, RHO, INVERSE, STIFF, THIRD, LEVEL, WEIGHT, LIVE = 0, 3, 4, 5, 6, 7, 15, 17
COEFS = (TILES, 25, MODES, LANES)


def spread(ref, t, row=0):
    lanes = pl.ds(t * LANES, LANES)
    part = ref[lanes].reshape(1, -1) if len(ref.shape) == 1 else ref[pl.ds(row, 1), lanes]
    return jnp.broadcast_to(part, (MODES, LANES))


def store_coefs(coefs, vel, den, snd, g2, orders):
    third = lax.broadcasted_iota(jnp.int32, (MODES, LANES), 0)
    for t in range(TILES):
        for k in range(3):
            coefs[t, FLOW + k] = spread(vel, t, k)
        rho, c = spread(den, t), spread(snd, t)
        coefs[t, RHO] = rho
        coefs[t, INVERSE] = 1.0 / rho
        coefs[t, STIFF] = rho * c * c
        coefs[t, THIRD] = spread(g2, t)
        order = jnp.broadcast_to(orders[pl.ds(t, 1)].reshape(1, 1), (MODES, LANES))
        for k in range(MODES):
            coefs[t, LEVEL + k] = jnp.where(jnp.maximum(third, k) <= order, 1.0, 0.0).astype(F32)
            coefs[t, LIVE + k] = jnp.where(order >= k, 1.0, 0.0).astype(F32)
        for parity in range(2):
            coefs[t, WEIGHT + parity] = sum(
                jnp.where(order >= m, m + 0.5, 0.0).astype(F32) for m in range(parity, MODES, 2)
            )


def medium(coefs, t):
    return [coefs[t, FLOW + k] for k in range(3)], coefs[t, RHO], coefs[t, INVERSE], coefs[t, STIFF]


def place():
    out = []
    for axis in ("dom", "grp"):
        i = lax.axis_index(axis)
        n = lax.axis_size(axis)
        sign = (1 - 2 * lax.rem(i, 2)).astype(F32)
        has = jnp.logical_and(i > 0, i < n - 1)
        out.append((sign, has))
    return out


def write_faces(d, sign, coef, sums, slots, t):
    us, rho, inv, stiff = coef
    half = 0.5 * sign
    u = half * us[d]
    near, far = HALF_WAVE + u, HALF_WAVE - u
    rho, inv, stiff = half * rho, half * inv, half * stiff

    for m in range(MODES):
        even = [sums[2 * d, f, rows(m), :] for f in range(FIELDS)]
        odd = [sign * sums[2 * d + 1, f, rows(m), :] for f in range(FIELDS)]
        one = flux([a + b for a, b in zip(even, odd)], d, near, rho, inv, stiff)
        two = flux([a - b for a, b in zip(even, odd)], d, far, -rho, -inv, -stiff)
        for f in range(FIELDS):
            slots[0][t, f, rows(m), :] = one[f]
            slots[1][t, f, rows(m), :] = two[f]


def halo_pair(slots, sign, has, t, f, m, scale):
    near = slots[0][t, f, rows(m), :]
    far = jnp.where(has, slots[1][t, f, rows(m), :], 0.0)
    return scale * (near + far), (scale * sign) * (near - far)


def first_faces(*refs):
    small, (modal, q0, coefs, x_even, x_odd, y_even, y_odd), (sums, sems, *held, small_sems) = refs[:5], refs[5:12], refs[12:]
    loads = [pltpu.make_async_copy(a, b, small_sems.at[i]) for i, (a, b) in enumerate(zip(small, held))]
    for load in loads:
        load.start()
    def copy(t, f):
        return pltpu.make_async_copy(modal.at[f, :, :, pl.ds(t * LANES, LANES)], q0.at[t, f], sems.at[t, f])

    for t in range(TILES):
        for f in range(FIELDS):
            copy(t, f).start()
    (sign_x, _), (sign_y, _) = place()
    for load in loads:
        load.wait()
    store_coefs(coefs, *held)

    for t in range(TILES):
        for f in range(FIELDS):
            copy(t, f).wait()
            e0 = [None] * MODES
            o0 = [None] * MODES
            for a in range(MODES):
                e1 = o1 = None
                for b in range(MODES):
                    q = coefs[t, LEVEL + max(a, b)] * q0[t, f, a, rows(b), :]
                    q0[t, f, a, rows(b), :] = q
                    if a % 2 == 0:
                        e0[b] = q if e0[b] is None else e0[b] + q
                    else:
                        o0[b] = q if o0[b] is None else o0[b] + q
                    if b % 2 == 0:
                        e1 = q if e1 is None else e1 + q
                    else:
                        o1 = q if o1 is None else o1 + q
                sums[2, f, rows(a), :] = e1
                sums[3, f, rows(a), :] = o1
            for b in range(MODES):
                sums[0, f, rows(b), :] = e0[b]
                sums[1, f, rows(b), :] = o0[b]
        coef = medium(coefs, t)
        for d, sign, slots in ((0, sign_x, (x_even, x_odd)), (1, sign_y, (y_even, y_odd))):
            write_faces(d, sign, coef, sums, slots, t)


def scaled(coef, d, s):
    us, rho, inv, stiff = coef
    return s * us[d], s * rho, s * inv, s * stiff


def bases(d, even, odd, us, k):
    a_odd = flux(odd, d, *us)
    a_even = flux(even, d, *us)
    return (
        [-0.5 * (x + k * e) for x, e in zip(a_odd, even)],
        [-0.5 * (x + k * o) for x, o in zip(a_even, odd)],
    )


def parity_sums(load):
    even, odd = load(0), load(1)
    for m in range(2, MODES, 2):
        even = [a + b for a, b in zip(even, load(m))]
        odd = [a + b for a, b in zip(odd, load(m + 1))]
    return even, odd


def sweep(d, load, even, odd, us, emit):
    run = [even, odd]
    for m in range(MODES):
        here = run[m % 2]
        emit(m, [(2.0 * m + 1.0) * a for a in here] if m else here)
        if m < MODES - 1:
            w = flux(load(m), d, *us)
            run[1 - m % 2] = [a + b for a, b in zip(run[1 - m % 2], w)]


def third_direction(q, acc, coefs, metric, h):
    lane = lax.broadcasted_iota(jnp.int32, (MODES, LANES), 1)
    first, last = lane == 0, lane == LANES - 1

    def line(a, carry):
        def loader(t):
            return lambda m: [q[t, f, a, strided(m), :] for f in range(FIELDS)]

        own, up, down = [], [], []
        for t in range(TILES):
            even, odd = parity_sums(loader(t))
            own.append((even, odd))
            us, rho, inv, stiff = medium(coefs, t)
            u = 0.5 * us[2]
            rho, inv, stiff = 0.5 * rho, 0.5 * inv, 0.5 * stiff
            upper = flux([x + y for x, y in zip(even, odd)], 2, HALF_WAVE + u, rho, inv, stiff)
            lower = flux([x - y for x, y in zip(even, odd)], 2, HALF_WAVE - u, -rho, -inv, -stiff)
            up.append([pltpu.roll(x, 1, 1) for x in upper])
            down.append([pltpu.roll(x, LANES - 1, 1) for x in lower])
        for t in range(TILES):
            s = h * coefs[t, THIRD]
            half = 0.5 * s
            us = scaled(medium(coefs, t), 2, s)
            base_e, base_o = bases(2, *own[t], us, 2.0 * HALF_WAVE * s)
            for f in range(FIELDS):
                prior = jnp.where(first, up[1 - t][f], up[t][f])
                after = jnp.where(last, down[1 - t][f], down[t][f])
                base_e[f] = base_e[f] + half * (after + prior)
                base_o[f] = base_o[f] + half * (after - prior)

            def emit(m, terms):
                for f in range(FIELDS):
                    acc[t, f, a, strided(m), :] = terms[f]

            sweep(2, loader(t), base_e, base_o, us, emit)
        return carry

    lax.fori_loop(0, MODES, line, 0)


def second_direction(q, acc, coefs, metric, h):
    for t in range(TILES):
        s = h * metric[1]
        us = scaled(medium(coefs, t), 1, s)

        def line(a, carry):
            def load(m):
                return [q[t, f, a, rows(m), :] for f in range(FIELDS)]

            even, odd = parity_sums(load)
            base_e, base_o = bases(1, even, odd, us, 2.0 * HALF_WAVE * s)

            def emit(m, terms):
                for f in range(FIELDS):
                    acc[t, f, a, rows(m), :] = acc[t, f, a, rows(m), :] + terms[f]

            sweep(1, load, base_e, base_o, us, emit)
            return carry

        lax.fori_loop(0, MODES, line, 0)


def first_direction(q, acc, coefs, metric, h, finish):
    for t in range(TILES):
        s = h * metric[0]
        us = scaled(medium(coefs, t), 0, s)

        def line(b, carry):
            def load(m):
                return [q[t, f, m, rows(b), :] for f in range(FIELDS)]

            even, odd = parity_sums(load)
            base_e, base_o = bases(0, even, odd, us, 2.0 * HALF_WAVE * s)

            kept = {}

            def emit(m, terms):
                finish(t, b, m, [acc[t, f, m, rows(b), :] + terms[f] for f in range(FIELDS)], kept)

            sweep(0, load, base_e, base_o, us, emit)
            return carry

        lax.fori_loop(0, MODES, line, 0)


def local_rate(coefs, g0, g1, q0, r1, traces, acc):
    metric = g0[0], g1[0]
    traces[pl.ds(2, 2)] = jnp.zeros((2,) + FACE, F32)
    third_direction(q0, acc, coefs, metric, TIME_STEP)
    second_direction(q0, acc, coefs, metric, TIME_STEP)

    def finish(t, b, a, totals, kept):
        level = coefs[t, LEVEL + jnp.maximum(a, b)]
        slot = 2 + lax.rem(b, 2)
        for f in range(FIELDS):
            rate = level * totals[f]
            r1[t, f, a, rows(b), :] = rate
            q = q0[t, f, a, rows(b), :] + SECTION_B1 * rate
            kept[a % 2, f] = q if a < 2 else kept[a % 2, f] + q
            traces[slot, t, f, rows(a), :] = traces[slot, t, f, rows(a), :] + q
        if a == MODES - 1:
            for (parity, f), total in kept.items():
                traces[parity, t, f, rows(b), :] = total

    first_direction(q0, acc, coefs, metric, TIME_STEP, finish)


def second_faces(coefs, g0, g1, traces, xo, xe, yo, ye, x_even, x_odd, y_even, y_odd, sums):
    metric = g0[0], g1[0]
    (sign_x, has_x), (sign_y, has_y) = place()
    sides = ((0, (xe, xo), sign_x, has_x), (1, (ye, yo), sign_y, has_y))

    for t in range(TILES):
        mask = [coefs[t, LEVEL + k] for k in range(MODES)]
        weights = [coefs[t, WEIGHT + parity] for parity in range(2)]
        scale = [SECTION_B1 * TIME_STEP * metric[d] for d in range(2)]

        for f in range(FIELDS):
            pairs = []
            across = []
            for d, slots, sign, has in sides:
                pair = [
                    [mask[m] * x for x in halo_pair(slots, sign, has, t, f, m, scale[d])] for m in range(MODES)
                ]
                pairs.append(pair)
                across.append(
                    [
                        [sum(pair[m][kind] for m in range(parity + 2, MODES, 2)) + pair[parity][kind] for parity in range(2)]
                        for kind in range(2)
                    ]
                )
            for d in range(2):
                for m in range(MODES):
                    heavy = (m + 0.5) * mask[m]
                    for parity in range(2):
                        sums[2 * d + parity, f, rows(m), :] = traces[2 * d + parity, t, f, rows(m), :] + (
                            weights[parity] * pairs[d][m][parity] + heavy * across[1 - d][m % 2][parity]
                        )
        coef = medium(coefs, t)
        for d, sign, slots in ((0, sign_x, (x_even, x_odd)), (1, sign_y, (y_even, y_odd))):
            write_faces(d, sign, coef, sums, slots, t)


def store_halos(halo, xe, xo, ye, yo, metric, s):
    (sign_x, has_x), (sign_y, has_y) = place()
    for d, slots, sign, has in ((0, (xe, xo), sign_x, has_x), (1, (ye, yo), sign_y, has_y)):
        for t in range(TILES):
            scale = s * metric[d]

            def one(f, carry):
                for m in range(MODES):
                    plus, minus = halo_pair(slots, sign, has, t, f, m, scale)
                    halo[d, 0, t, f, rows(m), :] = plus
                    halo[d, 1, t, f, rows(m), :] = minus
                return carry

            lax.fori_loop(0, FIELDS, one, 0)


def halo_term(halo, t, f, a, b, weight, kind):
    return (a + 0.5) * halo[0, a % 2, t, f, rows(b), :] + weight * halo[1, kind, t, f, rows(a), :]


def second_local(coefs, g0, g1, q0, r1, xo, xe, yo, ye, part, q1, acc, halo):
    metric = g0[0], g1[0]
    store_halos(halo, xe, xo, ye, yo, metric, TIME_STEP)
    for t in range(TILES):

        def column(b, carry):
            weight = b.astype(F32) + 0.5
            kind = lax.rem(b, 2)
            for a in range(MODES):
                level = coefs[t, LEVEL + jnp.maximum(a, b)]
                for f in range(FIELDS):
                    rate = r1[t, f, a, rows(b), :] + level * halo_term(halo, t, f, a, b, weight, kind)
                    q = q0[t, f, a, rows(b), :] + SECTION_B1 * rate
                    q1[t, f, a, rows(b), :] = q
                    part[t, f, a, rows(b), :] = q + (SECTION_B2 * SECTION_A2) * rate
            return carry

        lax.fori_loop(0, MODES, column, 0)
    third_direction(q1, acc, coefs, metric, SECTION_B2 * TIME_STEP)
    second_direction(q1, acc, coefs, metric, SECTION_B2 * TIME_STEP)

    def finish(t, b, a, totals, kept):
        level = coefs[t, LEVEL + jnp.maximum(a, b)]
        for f in range(FIELDS):
            part[t, f, a, rows(b), :] = part[t, f, a, rows(b), :] + level * totals[f]

    first_direction(q1, acc, coefs, metric, SECTION_B2 * TIME_STEP, finish)


def last_add(coefs, g0, g1, part, xo, xe, yo, ye, out, done, sems):
    metric = g0[0], g1[0]
    (sign_x, has_x), (sign_y, has_y) = place()
    sides = ((0, (xe, xo), sign_x, has_x), (1, (ye, yo), sign_y, has_y))

    def copy(t, f):
        lanes = pl.ds(pl.multiple_of(t * LANES, LANES), LANES)
        return pltpu.make_async_copy(done.at[t, f], out.at[f, :, :, lanes], sems.at[t, f])

    def tile(t, carry):
        mask = [coefs[t, LEVEL + k] for k in range(MODES)]
        weight = [(m + 0.5) * coefs[t, LIVE + m] for m in range(MODES)]

        def field(f, carry):
            first, second = (
                [
                    [mask[m] * x for x in halo_pair(slots, sign, has, t, f, m, SECTION_B2 * TIME_STEP * metric[d])]
                    for m in range(MODES)
                ]
                for d, slots, sign, has in sides
            )
            for a in range(MODES):
                for b in range(MODES):
                    term = weight[a] * first[b][a % 2] + weight[b] * second[a][b % 2]
                    done[t, f, a, rows(b), :] = part[t, f, a, rows(b), :] + term
            copy(t, f).start()
            return carry

        return lax.fori_loop(0, FIELDS, field, carry)

    lax.fori_loop(0, TILES, tile, 0)
    for t in range(TILES):
        for f in range(FIELDS):
            copy(t, f).wait()


SCALAR = pl.BlockSpec(memory_space=pltpu.SMEM)
LOCAL = pl.BlockSpec(memory_space=pltpu.VMEM)
FAR = pl.BlockSpec(memory_space=pltpu.HBM)


def call(body, operands, specs, outs, out_specs, scratch, cost):
    return pl.pallas_call(
        body,
        out_shape=outs,
        in_specs=specs,
        out_specs=out_specs,
        scratch_shapes=scratch,
        compiler_params=pltpu.CompilerParams(vmem_limit_bytes=VMEM_LIMIT),
        cost_estimate=pl.CostEstimate(flops=cost, bytes_accessed=2_600_000, transcendentals=0),
        name=body.__name__,
    )(*operands)


def exchange(dom_perms, grp_perms, faces):
    x_even, x_odd, y_even, y_odd = faces
    both = ("dom", "grp")
    return (
        lax.ppermute(x_odd, both, dom_perms[1]),
        lax.ppermute(x_even, "dom", dom_perms[0]),
        lax.ppermute(y_odd, "grp", grp_perms[1]),
        lax.ppermute(y_even, "grp", grp_perms[0]),
    )


def pair_swaps(n_dom, n_grp):
    even = lambda n: [(i, i ^ 1) for i in range(n)]
    other = lambda i: ((i - 1) ^ 1) + 1
    dom_odd = []
    for i in range(n_dom):
        for j in range(n_grp):
            if 0 < i < n_dom - 1:
                target = other(i) * n_grp + j
            else:
                target = i * n_grp + (j ^ 1)
            dom_odd.append((i * n_grp + j, target))
    grp_odd = [(j, other(j) if 0 < j < n_grp - 1 else n_grp - 1 - j) for j in range(n_grp)]
    return (even(n_dom), dom_odd), (even(n_grp), grp_odd)


def per_device(n_dom, n_grp, modal, vel, den, snd, g0, g1, g2, orders):
    dom_perms, grp_perms = pair_swaps(n_dom, n_grp)
    swap = functools.partial(exchange, dom_perms, grp_perms)
    shape = modal.shape
    modal = modal.reshape(FIELDS, MODES, MODES * MODES, TILES * LANES)
    small = [vel, den, snd, g2, orders]
    face = jax.ShapeDtypeStruct(FACE, F32)
    bulk = jax.ShapeDtypeStruct(BULK, F32)
    sems = pltpu.SemaphoreType.DMA((TILES, FIELDS))
    plane = (FIELDS, MODES * MODES, LANES)
    q0, coefs, *faces = call(
        first_faces,
        tuple(pltpu.with_memory_space_constraint(x, pltpu.HBM) for x in (*small, modal)),
        [FAR] * 6,
        (bulk, jax.ShapeDtypeStruct(COEFS, F32)) + (face,) * 4,
        (LOCAL,) * 6,
        [pltpu.VMEM((4,) + plane, F32), sems]
        + [pltpu.VMEM(x.shape, x.dtype) for x in small]
        + [pltpu.SemaphoreType.DMA((len(small),))],
        2_000_000,
    )
    halos = swap(faces)
    r1, traces = call(
        local_rate,
        (coefs, g0, g1, q0),
        [LOCAL, SCALAR, SCALAR, LOCAL],
        (bulk, jax.ShapeDtypeStruct((4,) + FACE, F32)),
        (LOCAL,) * 2,
        [pltpu.VMEM(BULK, F32)],
        16_000_000,
    )
    faces = call(
        second_faces,
        (coefs, g0, g1, traces, *halos),
        [LOCAL, SCALAR, SCALAR] + [LOCAL] * 5,
        (face,) * 4,
        (LOCAL,) * 4,
        [pltpu.VMEM((4,) + plane, F32)],
        2_000_000,
    )
    last = swap(faces)
    halo = pltpu.VMEM((2, 2) + FACE, F32)
    part = call(
        second_local,
        (coefs, g0, g1, q0, r1, *halos),
        [LOCAL, SCALAR, SCALAR] + [LOCAL] * 6,
        bulk,
        LOCAL,
        [pltpu.VMEM(BULK, F32), pltpu.VMEM(BULK, F32), halo],
        20_000_000,
    )
    out = call(
        last_add,
        (coefs, g0, g1, part, *last),
        [LOCAL, SCALAR, SCALAR] + [LOCAL] * 5,
        jax.ShapeDtypeStruct(modal.shape, F32),
        FAR,
        [pltpu.VMEM(BULK, F32), sems],
        4_000_000,
    )
    return out.reshape(shape)


def solution(mesh):
    placed = (
        P(None, None, None, None, ("dom", "grp")),
        P(None, ("dom", "grp")),
        P(("dom", "grp")),
        P(("dom", "grp")),
        P("dom"),
        P("grp"),
        P(),
        P(("dom", "grp")),
    )
    return jax.shard_map(
        functools.partial(per_device, mesh.shape["dom"], mesh.shape["grp"]),
        mesh=mesh,
        in_specs=placed,
        out_specs=P(None, None, None, None, ("dom", "grp")),
        check_vma=False,
    )
```

```python
import functools

import jax
import jax.numpy as jnp
from jax import lax
from jax.experimental import pallas as pl
from jax.experimental.pallas import tpu as pltpu
from jax.sharding import PartitionSpec as P

HALF_WAVE = 1.25
TIME_STEP = 0.01
SECTION_A2 = -0.4178904745
SECTION_B1 = 0.1496590219993
SECTION_B2 = 0.3792103129999
MODES = 8
FIELDS = 5
LANES = 128
TILES = 2
FACE = (TILES, FIELDS, MODES * MODES, LANES)
BULK = (TILES, FIELDS, MODES, MODES * MODES, LANES)
F32 = jnp.float32
VMEM_LIMIT = 24 * 1024 * 1024


def rows(m):
    if isinstance(m, int):
        return pl.ds(m * MODES, MODES)
    return pl.ds(pl.multiple_of(m * MODES, MODES), MODES)


def strided(m):
    return pl.ds(m, MODES, stride=MODES)


def flux(q, d, u, rho, inv, stiff):
    n = q[1 + d]
    out = [u * q[0] + rho * n, u * q[1], u * q[2], u * q[3], u * q[4] + stiff * n]
    out[1 + d] = out[1 + d] + inv * q[4]
    return out


FLOW, RHO, INVERSE, STIFF, THIRD, LEVEL, WEIGHT, LIVE = 0, 3, 4, 5, 6, 7, 15, 17
COEFS = (TILES, 25, MODES, LANES)


def spread(ref, t, row=0):
    lanes = pl.ds(t * LANES, LANES)
    part = ref[lanes].reshape(1, -1) if len(ref.shape) == 1 else ref[pl.ds(row, 1), lanes]
    return jnp.broadcast_to(part, (MODES, LANES))


def store_coefs(coefs, vel, den, snd, g2, orders):
    third = lax.broadcasted_iota(jnp.int32, (MODES, LANES), 0)
    for t in range(TILES):
        for k in range(3):
            coefs[t, FLOW + k] = spread(vel, t, k)
        rho, c = spread(den, t), spread(snd, t)
        coefs[t, RHO] = rho
        coefs[t, INVERSE] = 1.0 / rho
        coefs[t, STIFF] = rho * c * c
        coefs[t, THIRD] = spread(g2, t)
        order = jnp.broadcast_to(orders[pl.ds(t, 1)].reshape(1, 1), (MODES, LANES))
        for k in range(MODES):
            coefs[t, LEVEL + k] = jnp.where(jnp.maximum(third, k) <= order, 1.0, 0.0).astype(F32)
            coefs[t, LIVE + k] = jnp.where(order >= k, 1.0, 0.0).astype(F32)
        for parity in range(2):
            coefs[t, WEIGHT + parity] = sum(
                jnp.where(order >= m, m + 0.5, 0.0).astype(F32) for m in range(parity, MODES, 2)
            )


def medium(coefs, t):
    return [coefs[t, FLOW + k] for k in range(3)], coefs[t, RHO], coefs[t, INVERSE], coefs[t, STIFF]


def place():
    out = []
    for axis in ("dom", "grp"):
        i = lax.axis_index(axis)
        n = lax.axis_size(axis)
        sign = (1 - 2 * lax.rem(i, 2)).astype(F32)
        has = jnp.logical_and(i > 0, i < n - 1)
        out.append((sign, has))
    return out


def write_faces(d, sign, coef, sums, slots, t):
    us, rho, inv, stiff = coef
    half = 0.5 * sign
    u = half * us[d]
    near, far = HALF_WAVE + u, HALF_WAVE - u
    rho, inv, stiff = half * rho, half * inv, half * stiff

    for m in range(MODES):
        even = [sums[2 * d, f, rows(m), :] for f in range(FIELDS)]
        odd = [sign * sums[2 * d + 1, f, rows(m), :] for f in range(FIELDS)]
        one = flux([a + b for a, b in zip(even, odd)], d, near, rho, inv, stiff)
        two = flux([a - b for a, b in zip(even, odd)], d, far, -rho, -inv, -stiff)
        for f in range(FIELDS):
            slots[0][t, f, rows(m), :] = one[f]
            slots[1][t, f, rows(m), :] = two[f]


def halo_sides(slots, has, t, f, masks, scale):
    out = []
    other = jnp.where(has, scale, 0.0)
    for m in range(MODES):
        near = (scale * masks[m]) * slots[0][t, f, rows(m), :]
        far = (other * masks[m]) * slots[1][t, f, rows(m), :]
        out.append([near + far, near - far])
    return out


def first_faces(*refs):
    small, (modal, q0, coefs, sums, x_even, x_odd, y_even, y_odd), (sems, *held, small_sems) = refs[:5], refs[5:13], refs[13:]
    def copy(t, f):
        return pltpu.make_async_copy(modal.at[f, :, :, pl.ds(t * LANES, LANES)], q0.at[t, f], sems.at[t, f])

    for f in range(FIELDS):
        copy(0, f).start()
    loads = [pltpu.make_async_copy(a, b, small_sems.at[i]) for i, (a, b) in enumerate(zip(small, held))]
    for load in loads:
        load.start()
    for f in range(FIELDS):
        copy(1, f).start()
    (sign_x, _), (sign_y, _) = place()
    for load in loads:
        load.wait()
    store_coefs(coefs, *held)

    for t in range(TILES):
        for f in range(FIELDS):
            copy(t, f).wait()
            e0 = [None] * MODES
            o0 = [None] * MODES
            for a in range(MODES):
                e1 = o1 = None
                for b in range(MODES):
                    q = coefs[t, LEVEL + max(a, b)] * q0[t, f, a, rows(b), :]
                    q0[t, f, a, rows(b), :] = q
                    if a % 2 == 0:
                        e0[b] = q if e0[b] is None else e0[b] + q
                    else:
                        o0[b] = q if o0[b] is None else o0[b] + q
                    if b % 2 == 0:
                        e1 = q if e1 is None else e1 + q
                    else:
                        o1 = q if o1 is None else o1 + q
                sums[2, t, f, rows(a), :] = e1
                sums[3, t, f, rows(a), :] = o1
            for b in range(MODES):
                sums[0, t, f, rows(b), :] = e0[b]
                sums[1, t, f, rows(b), :] = o0[b]
        coef = medium(coefs, t)
        for d, sign, slots in ((0, sign_x, (x_even, x_odd)), (1, sign_y, (y_even, y_odd))):
            write_faces(d, sign, coef, sums.at[:, t], slots, t)


def scaled(coef, d, s):
    us, rho, inv, stiff = coef
    return s * us[d], s * rho, s * inv, s * stiff


def bases(d, even, odd, us, k):
    a_odd = flux(odd, d, *us)
    a_even = flux(even, d, *us)
    return (
        [-0.5 * (x + k * e) for x, e in zip(a_odd, even)],
        [-0.5 * (x + k * o) for x, o in zip(a_even, odd)],
    )


def parity_sums(load):
    even, odd = load(0), load(1)
    for m in range(2, MODES, 2):
        even = [a + b for a, b in zip(even, load(m))]
        odd = [a + b for a, b in zip(odd, load(m + 1))]
    return even, odd


def sweep(d, load, even, odd, us, emit):
    run = [even, odd]
    for m in range(MODES):
        here = run[m % 2]
        emit(m, [(2.0 * m + 1.0) * a for a in here] if m else here)
        if m < MODES - 1:
            w = flux(load(m), d, *us)
            run[1 - m % 2] = [a + b for a, b in zip(run[1 - m % 2], w)]


def third_direction(q, acc, coefs, metric, h):
    lane = lax.broadcasted_iota(jnp.int32, (MODES, LANES), 1)
    first, last = lane == 0, lane == LANES - 1

    def line(a, carry):
        def loader(t):
            return lambda m: [q[t, f, a, strided(m), :] for f in range(FIELDS)]

        own, up, down = [], [], []
        for t in range(TILES):
            even, odd = parity_sums(loader(t))
            own.append((even, odd))
            us, rho, inv, stiff = medium(coefs, t)
            u = 0.5 * us[2]
            rho, inv, stiff = 0.5 * rho, 0.5 * inv, 0.5 * stiff
            upper = flux([x + y for x, y in zip(even, odd)], 2, HALF_WAVE + u, rho, inv, stiff)
            lower = flux([x - y for x, y in zip(even, odd)], 2, HALF_WAVE - u, -rho, -inv, -stiff)
            up.append([pltpu.roll(x, 1, 1) for x in upper])
            down.append([pltpu.roll(x, LANES - 1, 1) for x in lower])
        for t in range(TILES):
            s = h * coefs[t, THIRD]
            half = 0.5 * s
            us = scaled(medium(coefs, t), 2, s)
            base_e, base_o = bases(2, *own[t], us, 2.0 * HALF_WAVE * s)
            for f in range(FIELDS):
                prior = jnp.where(first, up[1 - t][f], up[t][f])
                after = jnp.where(last, down[1 - t][f], down[t][f])
                base_e[f] = base_e[f] + half * (after + prior)
                base_o[f] = base_o[f] + half * (after - prior)

            def emit(m, terms):
                for f in range(FIELDS):
                    acc[t, f, a, strided(m), :] = terms[f]

            sweep(2, loader(t), base_e, base_o, us, emit)
        return carry

    lax.fori_loop(0, MODES, line, 0, unroll=2)


def second_direction(q, acc, coefs, metric, h):
    for t in range(TILES):
        s = h * metric[1]
        us = scaled(medium(coefs, t), 1, s)

        def line(a, carry):
            def load(m):
                return [q[t, f, a, rows(m), :] for f in range(FIELDS)]

            even, odd = parity_sums(load)
            base_e, base_o = bases(1, even, odd, us, 2.0 * HALF_WAVE * s)

            def emit(m, terms):
                for f in range(FIELDS):
                    acc[t, f, a, rows(m), :] = acc[t, f, a, rows(m), :] + terms[f]

            sweep(1, load, base_e, base_o, us, emit)
            return carry

        lax.fori_loop(0, MODES, line, 0, unroll=2)


def first_direction(q, acc, coefs, metric, h, finish):
    for t in range(TILES):
        s = h * metric[0]
        us = scaled(medium(coefs, t), 0, s)

        def line(b, carry):
            def load(m):
                return [q[t, f, m, rows(b), :] for f in range(FIELDS)]

            even, odd = parity_sums(load)
            base_e, base_o = bases(0, even, odd, us, 2.0 * HALF_WAVE * s)

            kept = {}

            def emit(m, terms):
                finish(t, b, m, [acc[t, f, m, rows(b), :] + terms[f] for f in range(FIELDS)], kept)

            sweep(0, load, base_e, base_o, us, emit)
            return carry

        lax.fori_loop(0, MODES, line, 0, unroll=2)


def local_rate(coefs, g0, g1, sums, q0, r1, traces, acc):
    metric = g0[0], g1[0]
    third_direction(q0, acc, coefs, metric, TIME_STEP)
    second_direction(q0, acc, coefs, metric, TIME_STEP)

    def finish(t, b, a, totals, kept):
        level = coefs[t, LEVEL + jnp.maximum(a, b)]
        for f in range(FIELDS):
            rate = level * totals[f]
            r1[t, f, a, rows(b), :] = rate
            kept[a % 2, f] = rate if a < 2 else kept[a % 2, f] + rate
        if a == MODES - 1:
            for (parity, f), total in kept.items():
                traces[parity, t, f, rows(b), :] = sums[parity, t, f, rows(b), :] + SECTION_B1 * total

    first_direction(q0, acc, coefs, metric, TIME_STEP, finish)
    for t in range(TILES):

        def field(f, carry):
            for a in range(MODES):
                for parity in range(2):
                    total = r1[t, f, a, rows(parity), :]
                    for b in range(parity + 2, MODES, 2):
                        total = total + r1[t, f, a, rows(b), :]
                    traces[2 + parity, t, f, rows(a), :] = sums[2 + parity, t, f, rows(a), :] + SECTION_B1 * total
            return carry

        lax.fori_loop(0, FIELDS, field, 0)


def second_faces(coefs, g0, g1, traces, xo, xe, yo, ye, x_even, x_odd, y_even, y_odd, sums):
    (sign_x, has_x), (sign_y, has_y) = place()
    s = SECTION_B1 * TIME_STEP
    sides = (((xe, xo), has_x, s * g0[0]), ((ye, yo), has_y, s * g1[0]))
    signs = (sign_x, sign_y)
    for t in range(TILES):
        mask = [coefs[t, LEVEL + k] for k in range(MODES)]
        weights = [[coefs[t, WEIGHT], signs[d] * coefs[t, WEIGHT + 1]] for d in range(2)]
        heavy = [[(m + 0.5) * mask[m] * (signs[1 - d] if m % 2 else 1.0) for m in range(MODES)] for d in range(2)]
        for f in range(FIELDS):
            pairs = [halo_sides(slots, has, t, f, mask, scale) for slots, has, scale in sides]
            across = [
                [
                    [sum((pair[m][kind] for m in range(parity + 2, MODES, 2)), pair[parity][kind]) for parity in range(2)]
                    for kind in range(2)
                ]
                for pair in pairs
            ]
            for d in range(2):
                for m in range(MODES):
                    for parity in range(2):
                        sums[2 * d + parity, f, rows(m), :] = traces[2 * d + parity, t, f, rows(m), :] + (
                            weights[d][parity] * pairs[d][m][parity] + heavy[d][m] * across[1 - d][m % 2][parity]
                        )
        coef = medium(coefs, t)
        for d, slots in ((0, (x_even, x_odd)), (1, (y_even, y_odd))):
            write_faces(d, signs[d], coef, sums, slots, t)


def halo_terms(coefs, t, f, sides):
    mask = [coefs[t, LEVEL + k] for k in range(MODES)]
    plain = [(m + 0.5) * coefs[t, LIVE + m] for m in range(MODES)]
    first, second = (halo_sides(slots, has, t, f, mask, scale) for slots, has, scale, _ in sides)
    weights = [[(sides[d][3] if m % 2 else 1.0) * plain[m] for m in range(MODES)] for d in range(2)]
    return lambda a, b: weights[0][a] * first[b][a % 2] + weights[1][b] * second[a][b % 2]


def second_local(coefs, g0, g1, q0, r1, xo, xe, yo, ye, part, q1, acc):
    metric = g0[0], g1[0]
    (sign_x, has_x), (sign_y, has_y) = place()
    sides = (((xe, xo), has_x, TIME_STEP * metric[0], sign_x), ((ye, yo), has_y, TIME_STEP * metric[1], sign_y))
    for t in range(TILES):

        def field(f, carry):
            term = halo_terms(coefs, t, f, sides)
            for a in range(MODES):
                for b in range(MODES):
                    rate = r1[t, f, a, rows(b), :] + term(a, b)
                    q = q0[t, f, a, rows(b), :] + SECTION_B1 * rate
                    q1[t, f, a, rows(b), :] = q
                    part[t, f, a, rows(b), :] = q + (SECTION_B2 * SECTION_A2) * rate
            return carry

        lax.fori_loop(0, FIELDS, field, 0)
    third_direction(q1, acc, coefs, metric, SECTION_B2 * TIME_STEP)
    second_direction(q1, acc, coefs, metric, SECTION_B2 * TIME_STEP)

    def finish(t, b, a, totals, kept):
        level = coefs[t, LEVEL + jnp.maximum(a, b)]
        for f in range(FIELDS):
            part[t, f, a, rows(b), :] = part[t, f, a, rows(b), :] + level * totals[f]

    first_direction(q1, acc, coefs, metric, SECTION_B2 * TIME_STEP, finish)


def last_add(coefs, g0, g1, part, xo, xe, yo, ye, out, done, sems):
    (sign_x, has_x), (sign_y, has_y) = place()
    s = SECTION_B2 * TIME_STEP
    sides = (((xe, xo), has_x, s * g0[0], sign_x), ((ye, yo), has_y, s * g1[0], sign_y))

    def copy(t, f):
        lanes = pl.ds(pl.multiple_of(t * LANES, LANES), LANES)
        return pltpu.make_async_copy(done.at[t, f], out.at[f, :, :, lanes], sems.at[t, f])

    def tile(t, carry):
        def field(f, carry):
            term = halo_terms(coefs, t, f, sides)
            for a in range(MODES):
                for b in range(MODES):
                    done[t, f, a, rows(b), :] = part[t, f, a, rows(b), :] + term(a, b)
            copy(t, f).start()
            return carry

        return lax.fori_loop(0, FIELDS, field, carry)

    lax.fori_loop(0, TILES, tile, 0)
    for t in range(TILES):
        for f in range(FIELDS):
            copy(t, f).wait()


SCALAR = pl.BlockSpec(memory_space=pltpu.SMEM)
LOCAL = pl.BlockSpec(memory_space=pltpu.VMEM)
FAR = pl.BlockSpec(memory_space=pltpu.HBM)


def call(body, operands, specs, outs, out_specs, scratch, cost):
    return pl.pallas_call(
        body,
        out_shape=outs,
        in_specs=specs,
        out_specs=out_specs,
        scratch_shapes=scratch,
        compiler_params=pltpu.CompilerParams(vmem_limit_bytes=VMEM_LIMIT),
        cost_estimate=pl.CostEstimate(flops=cost, bytes_accessed=2_600_000, transcendentals=0),
        name=body.__name__,
    )(*operands)


def exchange(dom_perms, grp_perms, faces):
    x_even, x_odd, y_even, y_odd = faces
    both = ("dom", "grp")
    return (
        lax.ppermute(x_odd, both, dom_perms[1]),
        lax.ppermute(x_even, "dom", dom_perms[0]),
        lax.ppermute(y_odd, "grp", grp_perms[1]),
        lax.ppermute(y_even, "grp", grp_perms[0]),
    )


def pair_swaps(n_dom, n_grp):
    even = lambda n: [(i, i ^ 1) for i in range(n)]
    other = lambda i: ((i - 1) ^ 1) + 1
    dom_odd = []
    for i in range(n_dom):
        for j in range(n_grp):
            if 0 < i < n_dom - 1:
                target = other(i) * n_grp + j
            else:
                target = i * n_grp + (j ^ 1)
            dom_odd.append((i * n_grp + j, target))
    grp_odd = [(j, other(j) if 0 < j < n_grp - 1 else n_grp - 1 - j) for j in range(n_grp)]
    return (even(n_dom), dom_odd), (even(n_grp), grp_odd)


def per_device(n_dom, n_grp, modal, vel, den, snd, g0, g1, g2, orders):
    dom_perms, grp_perms = pair_swaps(n_dom, n_grp)
    swap = functools.partial(exchange, dom_perms, grp_perms)
    shape = modal.shape
    modal = modal.reshape(FIELDS, MODES, MODES * MODES, TILES * LANES)
    small = [vel, den, snd, g2, orders]
    face = jax.ShapeDtypeStruct(FACE, F32)
    bulk = jax.ShapeDtypeStruct(BULK, F32)
    sems = pltpu.SemaphoreType.DMA((TILES, FIELDS))
    plane = (FIELDS, MODES * MODES, LANES)
    q0, coefs, sums, *faces = call(
        first_faces,
        tuple(pltpu.with_memory_space_constraint(x, pltpu.HBM) for x in (*small, modal)),
        [FAR] * 6,
        (bulk, jax.ShapeDtypeStruct(COEFS, F32), jax.ShapeDtypeStruct((4,) + FACE, F32)) + (face,) * 4,
        (LOCAL,) * 7,
        [sems]
        + [pltpu.VMEM(x.shape, x.dtype) for x in small]
        + [pltpu.SemaphoreType.DMA((len(small),))],
        2_000_000,
    )
    halos = swap(faces)
    r1, traces = call(
        local_rate,
        (coefs, g0, g1, sums, q0),
        [LOCAL, SCALAR, SCALAR, LOCAL, LOCAL],
        (bulk, jax.ShapeDtypeStruct((4,) + FACE, F32)),
        (LOCAL,) * 2,
        [pltpu.VMEM(BULK, F32)],
        16_000_000,
    )
    faces = call(
        second_faces,
        (coefs, g0, g1, traces, *halos),
        [LOCAL, SCALAR, SCALAR] + [LOCAL] * 5,
        (face,) * 4,
        (LOCAL,) * 4,
        [pltpu.VMEM((4,) + plane, F32)],
        2_000_000,
    )
    last = swap(faces)
    part = call(
        second_local,
        (coefs, g0, g1, q0, r1, *halos),
        [LOCAL, SCALAR, SCALAR] + [LOCAL] * 6,
        bulk,
        LOCAL,
        [pltpu.VMEM(BULK, F32), pltpu.VMEM(BULK, F32)],
        20_000_000,
    )
    out = call(
        last_add,
        (coefs, g0, g1, part, *last),
        [LOCAL, SCALAR, SCALAR] + [LOCAL] * 5,
        jax.ShapeDtypeStruct(modal.shape, F32),
        FAR,
        [pltpu.VMEM(BULK, F32), sems],
        4_000_000,
    )
    return out.reshape(shape)


def solution(mesh):
    placed = (
        P(None, None, None, None, ("dom", "grp")),
        P(None, ("dom", "grp")),
        P(("dom", "grp")),
        P(("dom", "grp")),
        P("dom"),
        P("grp"),
        P(),
        P(("dom", "grp")),
    )
    return jax.shard_map(
        functools.partial(per_device, mesh.shape["dom"], mesh.shape["grp"]),
        mesh=mesh,
        in_specs=placed,
        out_specs=P(None, None, None, None, ("dom", "grp")),
        check_vma=False,
    )
```

```python
import functools

import jax
import jax.numpy as jnp
from jax import lax
from jax.experimental import pallas as pl
from jax.experimental.pallas import tpu as pltpu
from jax.sharding import PartitionSpec as P

HALF_WAVE = 1.25
TIME_STEP = 0.01
SECTION_A2 = -0.4178904745
SECTION_B1 = 0.1496590219993
SECTION_B2 = 0.3792103129999
MODES = 8
FIELDS = 5
LANES = 128
TILES = 2
FACE = (TILES, FIELDS, MODES * MODES, LANES)
BULK = (TILES, FIELDS, MODES, MODES * MODES, LANES)
F32 = jnp.float32
VMEM_LIMIT = 24 * 1024 * 1024


def rows(m):
    if isinstance(m, int):
        return pl.ds(m * MODES, MODES)
    return pl.ds(pl.multiple_of(m * MODES, MODES), MODES)


def strided(m):
    return pl.ds(m, MODES, stride=MODES)


def flux(q, d, u, rho, inv, stiff):
    n = q[1 + d]
    out = [u * q[0] + rho * n, u * q[1], u * q[2], u * q[3], u * q[4] + stiff * n]
    out[1 + d] = out[1 + d] + inv * q[4]
    return out


FLOW, RHO, INVERSE, STIFF, THIRD, LEVEL, WEIGHT, LIVE = 0, 3, 4, 5, 6, 7, 15, 17
COEFS = (TILES, 25, MODES, LANES)


def spread(ref, t, row=0):
    lanes = pl.ds(t * LANES, LANES)
    part = ref[lanes].reshape(1, -1) if len(ref.shape) == 1 else ref[pl.ds(row, 1), lanes]
    return jnp.broadcast_to(part, (MODES, LANES))


def store_coefs(coefs, vel, den, snd, g2, orders):
    third = lax.broadcasted_iota(jnp.int32, (MODES, LANES), 0)
    for t in range(TILES):
        for k in range(3):
            coefs[t, FLOW + k] = spread(vel, t, k)
        rho, c = spread(den, t), spread(snd, t)
        coefs[t, RHO] = rho
        coefs[t, INVERSE] = 1.0 / rho
        coefs[t, STIFF] = rho * c * c
        coefs[t, THIRD] = spread(g2, t)
        order = jnp.broadcast_to(orders[pl.ds(t, 1)].reshape(1, 1), (MODES, LANES))
        for k in range(MODES):
            coefs[t, LEVEL + k] = jnp.where(jnp.maximum(third, k) <= order, 1.0, 0.0).astype(F32)
            coefs[t, LIVE + k] = jnp.where(order >= k, 1.0, 0.0).astype(F32)
        for parity in range(2):
            coefs[t, WEIGHT + parity] = sum(
                jnp.where(order >= m, m + 0.5, 0.0).astype(F32) for m in range(parity, MODES, 2)
            )


def medium(coefs, t):
    return [coefs[t, FLOW + k] for k in range(3)], coefs[t, RHO], coefs[t, INVERSE], coefs[t, STIFF]


def place():
    out = []
    for axis in ("dom", "grp"):
        i = lax.axis_index(axis)
        n = lax.axis_size(axis)
        sign = (1 - 2 * lax.rem(i, 2)).astype(F32)
        has = jnp.logical_and(i > 0, i < n - 1)
        out.append((sign, has))
    return out


def write_faces(d, sign, coef, sums, slots, t):
    us, rho, inv, stiff = coef
    half = 0.5 * sign
    u = half * us[d]
    near, far = HALF_WAVE + u, HALF_WAVE - u
    rho, inv, stiff = half * rho, half * inv, half * stiff

    for m in range(MODES):
        even = [sums[2 * d, f, rows(m), :] for f in range(FIELDS)]
        odd = [sign * sums[2 * d + 1, f, rows(m), :] for f in range(FIELDS)]
        one = flux([a + b for a, b in zip(even, odd)], d, near, rho, inv, stiff)
        two = flux([a - b for a, b in zip(even, odd)], d, far, -rho, -inv, -stiff)
        for f in range(FIELDS):
            slots[0][t, f, rows(m), :] = one[f]
            slots[1][t, f, rows(m), :] = two[f]


def halo_sides(slots, has, t, f, masks, scale):
    out = []
    other = jnp.where(has, scale, 0.0)
    for m in range(MODES):
        near = (scale * masks[m]) * slots[0][t, f, rows(m), :]
        far = (other * masks[m]) * slots[1][t, f, rows(m), :]
        out.append([near + far, near - far])
    return out


def first_faces(*refs):
    small, (modal, q0, coefs, sums, x_even, x_odd), (sems, *held, small_sems) = refs[:5], refs[5:11], refs[11:]

    def copy(t, f):
        return pltpu.make_async_copy(modal.at[f, :, :, pl.ds(t * LANES, LANES)], q0.at[t, f], sems.at[t, f])

    for f in range(FIELDS):
        copy(0, f).start()
    loads = [pltpu.make_async_copy(a, b, small_sems.at[i]) for i, (a, b) in enumerate(zip(small, held))]
    for load in loads:
        load.start()
    for f in range(FIELDS):
        copy(1, f).start()
    (sign_x, _), _ = place()
    for load in loads:
        load.wait()
    store_coefs(coefs, *held)

    for t in range(TILES):
        for f in range(FIELDS):
            copy(t, f).wait()
            e0 = [None] * MODES
            o0 = [None] * MODES
            for a in range(MODES):
                e1 = o1 = None
                for b in range(MODES):
                    q = coefs[t, LEVEL + max(a, b)] * q0[t, f, a, rows(b), :]
                    q0[t, f, a, rows(b), :] = q
                    if a % 2 == 0:
                        e0[b] = q if e0[b] is None else e0[b] + q
                    else:
                        o0[b] = q if o0[b] is None else o0[b] + q
                    if b % 2 == 0:
                        e1 = q if e1 is None else e1 + q
                    else:
                        o1 = q if o1 is None else o1 + q
                sums[2, t, f, rows(a), :] = e1
                sums[3, t, f, rows(a), :] = o1
            for b in range(MODES):
                sums[0, t, f, rows(b), :] = e0[b]
                sums[1, t, f, rows(b), :] = o0[b]
        write_faces(0, sign_x, medium(coefs, t), sums.at[:, t], (x_even, x_odd), t)


def first_grp_faces(coefs, sums, y_even, y_odd):
    _, (sign_y, _) = place()
    for t in range(TILES):
        write_faces(1, sign_y, medium(coefs, t), sums.at[:, t], (y_even, y_odd), t)


def scaled(coef, d, s):
    us, rho, inv, stiff = coef
    return s * us[d], s * rho, s * inv, s * stiff


def bases(d, even, odd, us, k):
    a_odd = flux(odd, d, *us)
    a_even = flux(even, d, *us)
    return (
        [-0.5 * (x + k * e) for x, e in zip(a_odd, even)],
        [-0.5 * (x + k * o) for x, o in zip(a_even, odd)],
    )


def parity_sums(load):
    even, odd = load(0), load(1)
    for m in range(2, MODES, 2):
        even = [a + b for a, b in zip(even, load(m))]
        odd = [a + b for a, b in zip(odd, load(m + 1))]
    return even, odd


def sweep(d, load, even, odd, us, emit):
    run = [even, odd]
    for m in range(MODES):
        here = run[m % 2]
        emit(m, [(2.0 * m + 1.0) * a for a in here] if m else here)
        if m < MODES - 1:
            w = flux(load(m), d, *us)
            run[1 - m % 2] = [a + b for a, b in zip(run[1 - m % 2], w)]


def third_direction(q, acc, coefs, metric, h):
    lane = lax.broadcasted_iota(jnp.int32, (MODES, LANES), 1)
    first, last = lane == 0, lane == LANES - 1

    def line(a, carry):
        def loader(t):
            return lambda m: [q[t, f, a, strided(m), :] for f in range(FIELDS)]

        own, up, down = [], [], []
        for t in range(TILES):
            even, odd = parity_sums(loader(t))
            own.append((even, odd))
            us, rho, inv, stiff = medium(coefs, t)
            u = 0.5 * us[2]
            rho, inv, stiff = 0.5 * rho, 0.5 * inv, 0.5 * stiff
            upper = flux([x + y for x, y in zip(even, odd)], 2, HALF_WAVE + u, rho, inv, stiff)
            lower = flux([x - y for x, y in zip(even, odd)], 2, HALF_WAVE - u, -rho, -inv, -stiff)
            up.append([pltpu.roll(x, 1, 1) for x in upper])
            down.append([pltpu.roll(x, LANES - 1, 1) for x in lower])
        for t in range(TILES):
            s = h * coefs[t, THIRD]
            half = 0.5 * s
            us = scaled(medium(coefs, t), 2, s)
            base_e, base_o = bases(2, *own[t], us, 2.0 * HALF_WAVE * s)
            for f in range(FIELDS):
                prior = jnp.where(first, up[1 - t][f], up[t][f])
                after = jnp.where(last, down[1 - t][f], down[t][f])
                base_e[f] = base_e[f] + half * (after + prior)
                base_o[f] = base_o[f] + half * (after - prior)

            def emit(m, terms):
                for f in range(FIELDS):
                    acc[t, f, a, strided(m), :] = terms[f]

            sweep(2, loader(t), base_e, base_o, us, emit)
        return carry

    lax.fori_loop(0, MODES, line, 0, unroll=2)


def second_direction(q, acc, coefs, metric, h):
    for t in range(TILES):
        s = h * metric[1]
        us = scaled(medium(coefs, t), 1, s)

        def line(a, carry):
            def load(m):
                return [q[t, f, a, rows(m), :] for f in range(FIELDS)]

            even, odd = parity_sums(load)
            base_e, base_o = bases(1, even, odd, us, 2.0 * HALF_WAVE * s)

            def emit(m, terms):
                for f in range(FIELDS):
                    acc[t, f, a, rows(m), :] = acc[t, f, a, rows(m), :] + terms[f]

            sweep(1, load, base_e, base_o, us, emit)
            return carry

        lax.fori_loop(0, MODES, line, 0, unroll=2)


def first_direction(q, acc, coefs, metric, h, finish):
    for t in range(TILES):
        s = h * metric[0]
        us = scaled(medium(coefs, t), 0, s)

        def line(b, carry):
            def load(m):
                return [q[t, f, m, rows(b), :] for f in range(FIELDS)]

            even, odd = parity_sums(load)
            base_e, base_o = bases(0, even, odd, us, 2.0 * HALF_WAVE * s)

            kept = {}

            def emit(m, terms):
                finish(t, b, m, [acc[t, f, m, rows(b), :] + terms[f] for f in range(FIELDS)], kept)

            sweep(0, load, base_e, base_o, us, emit)
            return carry

        lax.fori_loop(0, MODES, line, 0, unroll=2)


def local_rate(coefs, g0, g1, sums, q0, r1, traces, acc):
    metric = g0[0], g1[0]
    third_direction(q0, acc, coefs, metric, TIME_STEP)
    second_direction(q0, acc, coefs, metric, TIME_STEP)

    def finish(t, b, a, totals, kept):
        level = coefs[t, LEVEL + jnp.maximum(a, b)]
        for f in range(FIELDS):
            rate = level * totals[f]
            r1[t, f, a, rows(b), :] = rate
            kept[a % 2, f] = rate if a < 2 else kept[a % 2, f] + rate
        if a == MODES - 1:
            for (parity, f), total in kept.items():
                traces[parity, t, f, rows(b), :] = sums[parity, t, f, rows(b), :] + SECTION_B1 * total

    first_direction(q0, acc, coefs, metric, TIME_STEP, finish)
    for t in range(TILES):

        def field(f, carry):
            for a in range(MODES):
                for parity in range(2):
                    total = r1[t, f, a, rows(parity), :]
                    for b in range(parity + 2, MODES, 2):
                        total = total + r1[t, f, a, rows(b), :]
                    traces[2 + parity, t, f, rows(a), :] = sums[2 + parity, t, f, rows(a), :] + SECTION_B1 * total
            return carry

        lax.fori_loop(0, FIELDS, field, 0)


def second_faces(d, coefs, g0, g1, traces, xo, xe, yo, ye, even, odd, sums, table=None):
    (sign_x, has_x), (sign_y, has_y) = place()
    s = SECTION_B1 * TIME_STEP
    sides = (((xe, xo), has_x, s * g0[0]), ((ye, yo), has_y, s * g1[0]))
    signs = (sign_x, sign_y)
    for t in range(TILES):
        mask = [coefs[t, LEVEL + k] for k in range(MODES)]
        live = coefs.at[t, pl.ds(WEIGHT, 2)] if table is None else table.at[t]
        weights = live[0], signs[d] * live[1]
        heavy = [(m + 0.5) * mask[m] * (signs[1 - d] if m % 2 else 1.0) for m in range(MODES)]
        for f in range(FIELDS):
            along, other = (
                halo_sides(slots, has, t, f, mask, scale) for slots, has, scale in (sides[d], sides[1 - d])
            )
            across = [
                [sum((other[m][kind] for m in range(parity + 2, MODES, 2)), other[parity][kind]) for parity in range(2)]
                for kind in range(2)
            ]
            for m in range(MODES):
                for parity in range(2):
                    sums[2 * d + parity, f, rows(m), :] = traces[2 * d + parity, t, f, rows(m), :] + (
                        weights[parity] * along[m][parity] + heavy[m] * across[m % 2][parity]
                    )
        write_faces(d, signs[d], medium(coefs, t), sums, (even, odd), t)


def second_dom_faces(*refs):
    *refs, weights, sums = refs
    for t in range(TILES):
        weights[t] = refs[0][t, pl.ds(WEIGHT, 2)]
    second_faces(0, *refs, sums)


def second_grp_faces(weights, *refs):
    second_faces(1, *refs, weights)


def halo_terms(coefs, t, f, sides):
    mask = [coefs[t, LEVEL + k] for k in range(MODES)]
    plain = [(m + 0.5) * coefs[t, LIVE + m] for m in range(MODES)]
    first, second = (halo_sides(slots, has, t, f, mask, scale) for slots, has, scale, _ in sides)
    weights = [[(sides[d][3] if m % 2 else 1.0) * plain[m] for m in range(MODES)] for d in range(2)]
    return lambda a, b: weights[0][a] * first[b][a % 2] + weights[1][b] * second[a][b % 2]


def second_local(coefs, g0, g1, q0, r1, xo, xe, yo, ye, part, q1, acc):
    metric = g0[0], g1[0]
    (sign_x, has_x), (sign_y, has_y) = place()
    sides = (((xe, xo), has_x, TIME_STEP * metric[0], sign_x), ((ye, yo), has_y, TIME_STEP * metric[1], sign_y))
    for t in range(TILES):

        def field(f, carry):
            term = halo_terms(coefs, t, f, sides)
            for a in range(MODES):
                for b in range(MODES):
                    rate = r1[t, f, a, rows(b), :] + term(a, b)
                    q = q0[t, f, a, rows(b), :] + SECTION_B1 * rate
                    q1[t, f, a, rows(b), :] = q
                    part[t, f, a, rows(b), :] = q + (SECTION_B2 * SECTION_A2) * rate
            return carry

        lax.fori_loop(0, FIELDS, field, 0)
    third_direction(q1, acc, coefs, metric, SECTION_B2 * TIME_STEP)
    second_direction(q1, acc, coefs, metric, SECTION_B2 * TIME_STEP)

    def finish(t, b, a, totals, kept):
        level = coefs[t, LEVEL + jnp.maximum(a, b)]
        for f in range(FIELDS):
            part[t, f, a, rows(b), :] = part[t, f, a, rows(b), :] + level * totals[f]

    first_direction(q1, acc, coefs, metric, SECTION_B2 * TIME_STEP, finish)


def last_add(coefs, g0, g1, part, xo, xe, yo, ye, out, done, sems):
    (sign_x, has_x), (sign_y, has_y) = place()
    s = SECTION_B2 * TIME_STEP
    sides = (((xe, xo), has_x, s * g0[0], sign_x), ((ye, yo), has_y, s * g1[0], sign_y))

    def copy(t, f):
        lanes = pl.ds(pl.multiple_of(t * LANES, LANES), LANES)
        return pltpu.make_async_copy(done.at[t, f], out.at[f, :, :, lanes], sems.at[t, f])

    def tile(t, carry):
        def field(f, carry):
            term = halo_terms(coefs, t, f, sides)
            for a in range(MODES):
                for b in range(MODES):
                    done[t, f, a, rows(b), :] = part[t, f, a, rows(b), :] + term(a, b)
            copy(t, f).start()
            return carry

        return lax.fori_loop(0, FIELDS, field, carry)

    lax.fori_loop(0, TILES, tile, 0)
    for t in range(TILES):
        for f in range(FIELDS):
            copy(t, f).wait()


SCALAR = pl.BlockSpec(memory_space=pltpu.SMEM)
LOCAL = pl.BlockSpec(memory_space=pltpu.VMEM)
FAR = pl.BlockSpec(memory_space=pltpu.HBM)


def call(body, operands, specs, outs, out_specs, scratch, cost):
    return pl.pallas_call(
        body,
        out_shape=outs,
        in_specs=specs,
        out_specs=out_specs,
        scratch_shapes=scratch,
        compiler_params=pltpu.CompilerParams(vmem_limit_bytes=VMEM_LIMIT),
        cost_estimate=pl.CostEstimate(flops=cost, bytes_accessed=2_600_000, transcendentals=0),
        name=body.__name__,
    )(*operands)


def exchange(dom_perms, grp_perms, faces):
    x_even, x_odd, y_even, y_odd = faces
    both = ("dom", "grp")
    return (
        lax.ppermute(x_odd, both, dom_perms[1]),
        lax.ppermute(x_even, "dom", dom_perms[0]),
        lax.ppermute(y_odd, "grp", grp_perms[1]),
        lax.ppermute(y_even, "grp", grp_perms[0]),
    )


def pair_swaps(n_dom, n_grp):
    even = lambda n: [(i, i ^ 1) for i in range(n)]
    other = lambda i: ((i - 1) ^ 1) + 1
    dom_odd = []
    for i in range(n_dom):
        for j in range(n_grp):
            if 0 < i < n_dom - 1:
                target = other(i) * n_grp + j
            else:
                target = i * n_grp + (j ^ 1)
            dom_odd.append((i * n_grp + j, target))
    grp_odd = [(j, other(j) if 0 < j < n_grp - 1 else n_grp - 1 - j) for j in range(n_grp)]
    return (even(n_dom), dom_odd), (even(n_grp), grp_odd)


def per_device(n_dom, n_grp, modal, vel, den, snd, g0, g1, g2, orders):
    dom_perms, grp_perms = pair_swaps(n_dom, n_grp)
    swap = functools.partial(exchange, dom_perms, grp_perms)
    shape = modal.shape
    modal = modal.reshape(FIELDS, MODES, MODES * MODES, TILES * LANES)
    small = [vel, den, snd, g2, orders]
    face = jax.ShapeDtypeStruct(FACE, F32)
    bulk = jax.ShapeDtypeStruct(BULK, F32)
    sems = pltpu.SemaphoreType.DMA((TILES, FIELDS))
    plane = (FIELDS, MODES * MODES, LANES)
    q0, coefs, sums, *x_faces = call(
        first_faces,
        tuple(pltpu.with_memory_space_constraint(x, pltpu.HBM) for x in (*small, modal)),
        [FAR] * 6,
        (bulk, jax.ShapeDtypeStruct(COEFS, F32), jax.ShapeDtypeStruct((4,) + FACE, F32)) + (face,) * 2,
        (LOCAL,) * 5,
        [sems]
        + [pltpu.VMEM(x.shape, x.dtype) for x in small]
        + [pltpu.SemaphoreType.DMA((len(small),))],
        2_000_000,
    )
    y_faces = call(first_grp_faces, (coefs, sums), [LOCAL] * 2, (face,) * 2, (LOCAL,) * 2, [], 200_000)
    halos = swap((*x_faces, *y_faces))
    r1, traces = call(
        local_rate,
        (coefs, g0, g1, sums, q0),
        [LOCAL, SCALAR, SCALAR, LOCAL, LOCAL],
        (bulk, jax.ShapeDtypeStruct((4,) + FACE, F32)),
        (LOCAL,) * 2,
        [pltpu.VMEM(BULK, F32)],
        16_000_000,
    )
    made = (coefs, g0, g1, traces, *halos)
    specs = [LOCAL, SCALAR, SCALAR] + [LOCAL] * 5
    work = [pltpu.VMEM((4,) + plane, F32)]
    *x_faces, weights = call(
        second_dom_faces,
        made,
        specs,
        (face, face, jax.ShapeDtypeStruct((TILES, 2, MODES, LANES), F32)),
        (LOCAL,) * 3,
        work,
        1_000_000,
    )
    y_faces = call(
        second_grp_faces, (weights, *made), [LOCAL] + specs, (face,) * 2, (LOCAL,) * 2, work, 1_000_000
    )
    last = swap((*x_faces, *y_faces))
    part = call(
        second_local,
        (coefs, g0, g1, q0, r1, *halos),
        [LOCAL, SCALAR, SCALAR] + [LOCAL] * 6,
        bulk,
        LOCAL,
        [pltpu.VMEM(BULK, F32), pltpu.VMEM(BULK, F32)],
        20_000_000,
    )
    out = call(
        last_add,
        (coefs, g0, g1, part, *last),
        [LOCAL, SCALAR, SCALAR] + [LOCAL] * 5,
        jax.ShapeDtypeStruct(modal.shape, F32),
        FAR,
        [pltpu.VMEM(BULK, F32), sems],
        4_000_000,
    )
    return out.reshape(shape)


def solution(mesh):
    placed = (
        P(None, None, None, None, ("dom", "grp")),
        P(None, ("dom", "grp")),
        P(("dom", "grp")),
        P(("dom", "grp")),
        P("dom"),
        P("grp"),
        P(),
        P(("dom", "grp")),
    )
    return jax.shard_map(
        functools.partial(per_device, mesh.shape["dom"], mesh.shape["grp"]),
        mesh=mesh,
        in_specs=placed,
        out_specs=P(None, None, None, None, ("dom", "grp")),
        check_vma=False,
    )
```

```python
import functools

import jax
import jax.numpy as jnp
from jax import lax
from jax.experimental import pallas as pl
from jax.experimental.pallas import tpu as pltpu
from jax.sharding import PartitionSpec as P

HALF_WAVE = 1.25
TIME_STEP = 0.01
SECTION_A2 = -0.4178904745
SECTION_B1 = 0.1496590219993
SECTION_B2 = 0.3792103129999
MODES = 8
FIELDS = 5
LANES = 128
TILES = 2
FACE = (TILES, FIELDS, MODES * MODES, LANES)
BULK = (TILES, FIELDS, MODES, MODES * MODES, LANES)
F32 = jnp.float32
VMEM_LIMIT = 24 * 1024 * 1024


def rows(m):
    if isinstance(m, int):
        return pl.ds(m * MODES, MODES)
    return pl.ds(pl.multiple_of(m * MODES, MODES), MODES)


def strided(m):
    return pl.ds(m, MODES, stride=MODES)


def flux(q, d, u, rho, inv, stiff):
    n = q[1 + d]
    out = [u * q[0] + rho * n, u * q[1], u * q[2], u * q[3], u * q[4] + stiff * n]
    out[1 + d] = out[1 + d] + inv * q[4]
    return out


FLOW, RHO, INVERSE, STIFF, THIRD, LEVEL, WEIGHT, LIVE = 0, 3, 4, 5, 6, 7, 15, 17
COEFS = (TILES, 25, MODES, LANES)


def spread(ref, t, row=0):
    lanes = pl.ds(t * LANES, LANES)
    part = ref[lanes].reshape(1, -1) if len(ref.shape) == 1 else ref[pl.ds(row, 1), lanes]
    return jnp.broadcast_to(part, (MODES, LANES))


def store_coefs(coefs, vel, den, snd, g2, orders):
    third = lax.broadcasted_iota(jnp.int32, (MODES, LANES), 0)
    for t in range(TILES):
        for k in range(3):
            coefs[t, FLOW + k] = spread(vel, t, k)
        rho, c = spread(den, t), spread(snd, t)
        coefs[t, RHO] = rho
        coefs[t, INVERSE] = 1.0 / rho
        coefs[t, STIFF] = rho * c * c
        coefs[t, THIRD] = spread(g2, t)
        order = jnp.broadcast_to(orders[pl.ds(t, 1)].reshape(1, 1), (MODES, LANES))
        for k in range(MODES):
            coefs[t, LEVEL + k] = jnp.where(jnp.maximum(third, k) <= order, 1.0, 0.0).astype(F32)
            coefs[t, LIVE + k] = jnp.where(order >= k, 1.0, 0.0).astype(F32)
        for parity in range(2):
            coefs[t, WEIGHT + parity] = sum(
                jnp.where(order >= m, m + 0.5, 0.0).astype(F32) for m in range(parity, MODES, 2)
            )


def medium(coefs, t):
    return [coefs[t, FLOW + k] for k in range(3)], coefs[t, RHO], coefs[t, INVERSE], coefs[t, STIFF]


def place():
    out = []
    for axis in ("dom", "grp"):
        i = lax.axis_index(axis)
        n = lax.axis_size(axis)
        sign = (1 - 2 * lax.rem(i, 2)).astype(F32)
        has = jnp.logical_and(i > 0, i < n - 1)
        out.append((sign, has))
    return out


def write_faces(d, sign, coef, sums, slots, t):
    us, rho, inv, stiff = coef
    half = 0.5 * sign
    u = half * us[d]
    near, far = HALF_WAVE + u, HALF_WAVE - u
    rho, inv, stiff = half * rho, half * inv, half * stiff

    for m in range(MODES):
        even = [sums[2 * d, f, rows(m), :] for f in range(FIELDS)]
        odd = [sign * sums[2 * d + 1, f, rows(m), :] for f in range(FIELDS)]
        one = flux([a + b for a, b in zip(even, odd)], d, near, rho, inv, stiff)
        two = flux([a - b for a, b in zip(even, odd)], d, far, -rho, -inv, -stiff)
        for f in range(FIELDS):
            slots[0][t, f, rows(m), :] = one[f]
            slots[1][t, f, rows(m), :] = two[f]


def halo_sides(slots, has, t, f, masks, scale):
    out = []
    other = jnp.where(has, scale, 0.0)
    for m in range(MODES):
        near = (scale * masks[m]) * slots[0][t, f, rows(m), :]
        far = (other * masks[m]) * slots[1][t, f, rows(m), :]
        out.append([near + far, near - far])
    return out


def first_faces(*refs):
    small, (modal, q0, coefs, sums, x_even, x_odd), (sems, *held, small_sems) = refs[:5], refs[5:11], refs[11:]

    def copy(t, f):
        return pltpu.make_async_copy(modal.at[f, :, :, pl.ds(t * LANES, LANES)], q0.at[t, f], sems.at[t, f])

    for f in range(FIELDS):
        copy(0, f).start()
    loads = [pltpu.make_async_copy(a, b, small_sems.at[i]) for i, (a, b) in enumerate(zip(small, held))]
    for load in loads:
        load.start()
    for f in range(FIELDS):
        copy(1, f).start()
    (sign_x, _), _ = place()
    for load in loads:
        load.wait()
    store_coefs(coefs, *held)

    for t in range(TILES):
        for f in range(FIELDS):
            copy(t, f).wait()
            e0 = [None] * MODES
            o0 = [None] * MODES
            for a in range(MODES):
                e1 = o1 = None
                for b in range(MODES):
                    q = coefs[t, LEVEL + max(a, b)] * q0[t, f, a, rows(b), :]
                    q0[t, f, a, rows(b), :] = q
                    if a % 2 == 0:
                        e0[b] = q if e0[b] is None else e0[b] + q
                    else:
                        o0[b] = q if o0[b] is None else o0[b] + q
                    if b % 2 == 0:
                        e1 = q if e1 is None else e1 + q
                    else:
                        o1 = q if o1 is None else o1 + q
                sums[2, t, f, rows(a), :] = e1
                sums[3, t, f, rows(a), :] = o1
            for b in range(MODES):
                sums[0, t, f, rows(b), :] = e0[b]
                sums[1, t, f, rows(b), :] = o0[b]
        write_faces(0, sign_x, medium(coefs, t), sums.at[:, t], (x_even, x_odd), t)


def first_grp_faces(coefs, sums, y_even, y_odd):
    _, (sign_y, _) = place()
    for t in range(TILES):
        write_faces(1, sign_y, medium(coefs, t), sums.at[:, t], (y_even, y_odd), t)


def scaled(coef, d, s):
    us, rho, inv, stiff = coef
    return s * us[d], s * rho, s * inv, s * stiff


def bases(d, even, odd, us, k):
    a_odd = flux(odd, d, *us)
    a_even = flux(even, d, *us)
    return (
        [-0.5 * (x + k * e) for x, e in zip(a_odd, even)],
        [-0.5 * (x + k * o) for x, o in zip(a_even, odd)],
    )


def parity_sums(load):
    even, odd = load(0), load(1)
    for m in range(2, MODES, 2):
        even = [a + b for a, b in zip(even, load(m))]
        odd = [a + b for a, b in zip(odd, load(m + 1))]
    return even, odd


def sweep(d, load, even, odd, us, emit):
    run = [even, odd]
    for m in range(MODES):
        here = run[m % 2]
        emit(m, [(2.0 * m + 1.0) * a for a in here] if m else here)
        if m < MODES - 1:
            w = flux(load(m), d, *us)
            run[1 - m % 2] = [a + b for a, b in zip(run[1 - m % 2], w)]


def third_direction(q, acc, coefs, metric, h):
    lane = lax.broadcasted_iota(jnp.int32, (MODES, LANES), 1)
    first, last = lane == 0, lane == LANES - 1

    def line(a, carry):
        def loader(t):
            return lambda m: [q[t, f, a, strided(m), :] for f in range(FIELDS)]

        own, up, down = [], [], []
        for t in range(TILES):
            even, odd = parity_sums(loader(t))
            own.append((even, odd))
            us, rho, inv, stiff = medium(coefs, t)
            u = 0.5 * us[2]
            rho, inv, stiff = 0.5 * rho, 0.5 * inv, 0.5 * stiff
            upper = flux([x + y for x, y in zip(even, odd)], 2, HALF_WAVE + u, rho, inv, stiff)
            lower = flux([x - y for x, y in zip(even, odd)], 2, HALF_WAVE - u, -rho, -inv, -stiff)
            up.append([pltpu.roll(x, 1, 1) for x in upper])
            down.append([pltpu.roll(x, LANES - 1, 1) for x in lower])
        for t in range(TILES):
            s = h * coefs[t, THIRD]
            half = 0.5 * s
            us = scaled(medium(coefs, t), 2, s)
            base_e, base_o = bases(2, *own[t], us, 2.0 * HALF_WAVE * s)
            for f in range(FIELDS):
                prior = jnp.where(first, up[1 - t][f], up[t][f])
                after = jnp.where(last, down[1 - t][f], down[t][f])
                base_e[f] = base_e[f] + half * (after + prior)
                base_o[f] = base_o[f] + half * (after - prior)

            def emit(m, terms):
                for f in range(FIELDS):
                    acc[t, f, a, strided(m), :] = terms[f]

            sweep(2, loader(t), base_e, base_o, us, emit)
        return carry

    lax.fori_loop(0, MODES, line, 0, unroll=2)


def second_direction(q, acc, coefs, metric, h):
    for t in range(TILES):
        s = h * metric[1]
        us = scaled(medium(coefs, t), 1, s)

        def line(a, carry):
            def load(m):
                return [q[t, f, a, rows(m), :] for f in range(FIELDS)]

            even, odd = parity_sums(load)
            base_e, base_o = bases(1, even, odd, us, 2.0 * HALF_WAVE * s)

            def emit(m, terms):
                for f in range(FIELDS):
                    acc[t, f, a, rows(m), :] = acc[t, f, a, rows(m), :] + terms[f]

            sweep(1, load, base_e, base_o, us, emit)
            return carry

        lax.fori_loop(0, MODES, line, 0, unroll=2)


def first_direction(q, acc, coefs, metric, h, finish):
    for t in range(TILES):
        s = h * metric[0]
        us = scaled(medium(coefs, t), 0, s)

        def line(b, carry):
            def load(m):
                return [q[t, f, m, rows(b), :] for f in range(FIELDS)]

            even, odd = parity_sums(load)
            base_e, base_o = bases(0, even, odd, us, 2.0 * HALF_WAVE * s)

            kept = {}

            def emit(m, terms):
                finish(t, b, m, [acc[t, f, m, rows(b), :] + terms[f] for f in range(FIELDS)], kept)

            sweep(0, load, base_e, base_o, us, emit)
            return carry

        lax.fori_loop(0, MODES, line, 0, unroll=2)


def local_rate(coefs, g0, g1, sums, q0, r1, traces, acc):
    metric = g0[0], g1[0]
    third_direction(q0, acc, coefs, metric, TIME_STEP)
    second_direction(q0, acc, coefs, metric, TIME_STEP)

    def finish(t, b, a, totals, kept):
        level = coefs[t, LEVEL + jnp.maximum(a, b)]
        for f in range(FIELDS):
            rate = level * totals[f]
            r1[t, f, a, rows(b), :] = rate
            kept[a % 2, f] = rate if a < 2 else kept[a % 2, f] + rate
        if a == MODES - 1:
            for (parity, f), total in kept.items():
                traces[parity, t, f, rows(b), :] = sums[parity, t, f, rows(b), :] + SECTION_B1 * total

    first_direction(q0, acc, coefs, metric, TIME_STEP, finish)
    for t in range(TILES):

        def field(f, carry):
            for a in range(MODES):
                for parity in range(2):
                    total = r1[t, f, a, rows(parity), :]
                    for b in range(parity + 2, MODES, 2):
                        total = total + r1[t, f, a, rows(b), :]
                    traces[2 + parity, t, f, rows(a), :] = sums[2 + parity, t, f, rows(a), :] + SECTION_B1 * total
            return carry

        lax.fori_loop(0, FIELDS, field, 0)


def second_faces(d, coefs, g0, g1, traces, xo, xe, yo, ye, even, odd, sums, table=None):
    (sign_x, has_x), (sign_y, has_y) = place()
    s = SECTION_B1 * TIME_STEP
    sides = (((xe, xo), has_x, s * g0[0]), ((ye, yo), has_y, s * g1[0]))
    signs = (sign_x, sign_y)
    for t in range(TILES):
        mask = [coefs[t, LEVEL + k] for k in range(MODES)]
        live = coefs.at[t, pl.ds(WEIGHT, 2)] if table is None else table.at[t]
        weights = live[0], signs[d] * live[1]
        heavy = [(m + 0.5) * mask[m] * (signs[1 - d] if m % 2 else 1.0) for m in range(MODES)]
        for f in range(FIELDS):
            along, other = (
                halo_sides(slots, has, t, f, mask, scale) for slots, has, scale in (sides[d], sides[1 - d])
            )
            across = [
                [sum((other[m][kind] for m in range(parity + 2, MODES, 2)), other[parity][kind]) for parity in range(2)]
                for kind in range(2)
            ]
            for m in range(MODES):
                for parity in range(2):
                    sums[2 * d + parity, f, rows(m), :] = traces[2 * d + parity, t, f, rows(m), :] + (
                        weights[parity] * along[m][parity] + heavy[m] * across[m % 2][parity]
                    )
        write_faces(d, signs[d], medium(coefs, t), sums, (even, odd), t)


def cross_terms(coefs, g1, traces, yo, ye, ready):
    _, (sign, has) = place()
    scale = SECTION_B1 * TIME_STEP * g1[0]
    for t in range(TILES):
        mask = [coefs[t, LEVEL + k] for k in range(MODES)]
        heavy = [(m + 0.5) * mask[m] * (sign if m % 2 else 1.0) for m in range(MODES)]
        for f in range(FIELDS):
            other = halo_sides((ye, yo), has, t, f, mask, scale)
            across = [
                [sum((other[m][kind] for m in range(parity + 2, MODES, 2)), other[parity][kind]) for parity in range(2)]
                for kind in range(2)
            ]
            for m in range(MODES):
                for parity in range(2):
                    ready[parity, t, f, rows(m), :] = (
                        traces[parity, t, f, rows(m), :] + heavy[m] * across[m % 2][parity]
                    )


def second_dom_faces(coefs, g0, ready, xo, xe, even, odd, weights, sums):
    (sign, has), _ = place()
    scale = SECTION_B1 * TIME_STEP * g0[0]
    for t in range(TILES):
        weights[t] = coefs[t, pl.ds(WEIGHT, 2)]
        mask = [coefs[t, LEVEL + k] for k in range(MODES)]
        weight = coefs[t, WEIGHT], sign * coefs[t, WEIGHT + 1]
        for f in range(FIELDS):
            along = halo_sides((xe, xo), has, t, f, mask, scale)
            for m in range(MODES):
                for parity in range(2):
                    sums[parity, f, rows(m), :] = ready[parity, t, f, rows(m), :] + weight[parity] * along[m][parity]
        write_faces(0, sign, medium(coefs, t), sums, (even, odd), t)


def second_grp_faces(weights, *refs):
    second_faces(1, *refs, weights)


def halo_terms(coefs, t, f, sides):
    mask = [coefs[t, LEVEL + k] for k in range(MODES)]
    plain = [(m + 0.5) * coefs[t, LIVE + m] for m in range(MODES)]
    first, second = (halo_sides(slots, has, t, f, mask, scale) for slots, has, scale, _ in sides)
    weights = [[(sides[d][3] if m % 2 else 1.0) * plain[m] for m in range(MODES)] for d in range(2)]
    return lambda a, b: weights[0][a] * first[b][a % 2] + weights[1][b] * second[a][b % 2]


def second_local(coefs, g0, g1, q0, r1, xo, xe, yo, ye, part, q1, acc):
    metric = g0[0], g1[0]
    (sign_x, has_x), (sign_y, has_y) = place()
    sides = (((xe, xo), has_x, TIME_STEP * metric[0], sign_x), ((ye, yo), has_y, TIME_STEP * metric[1], sign_y))
    for t in range(TILES):

        def field(f, carry):
            term = halo_terms(coefs, t, f, sides)
            for a in range(MODES):
                for b in range(MODES):
                    rate = r1[t, f, a, rows(b), :] + term(a, b)
                    q = q0[t, f, a, rows(b), :] + SECTION_B1 * rate
                    q1[t, f, a, rows(b), :] = q
                    part[t, f, a, rows(b), :] = q + (SECTION_B2 * SECTION_A2) * rate
            return carry

        lax.fori_loop(0, FIELDS, field, 0)
    third_direction(q1, acc, coefs, metric, SECTION_B2 * TIME_STEP)
    second_direction(q1, acc, coefs, metric, SECTION_B2 * TIME_STEP)

    def finish(t, b, a, totals, kept):
        level = coefs[t, LEVEL + jnp.maximum(a, b)]
        for f in range(FIELDS):
            part[t, f, a, rows(b), :] = part[t, f, a, rows(b), :] + level * totals[f]

    first_direction(q1, acc, coefs, metric, SECTION_B2 * TIME_STEP, finish)


def last_add(coefs, g0, g1, part, xo, xe, yo, ye, out, done, sems):
    (sign_x, has_x), (sign_y, has_y) = place()
    s = SECTION_B2 * TIME_STEP
    sides = (((xe, xo), has_x, s * g0[0], sign_x), ((ye, yo), has_y, s * g1[0], sign_y))

    def copy(t, f):
        lanes = pl.ds(pl.multiple_of(t * LANES, LANES), LANES)
        return pltpu.make_async_copy(done.at[t, f], out.at[f, :, :, lanes], sems.at[t, f])

    def tile(t, carry):
        def field(f, carry):
            term = halo_terms(coefs, t, f, sides)
            for a in range(MODES):
                for b in range(MODES):
                    done[t, f, a, rows(b), :] = part[t, f, a, rows(b), :] + term(a, b)
            copy(t, f).start()
            return carry

        return lax.fori_loop(0, FIELDS, field, carry)

    lax.fori_loop(0, TILES, tile, 0)
    for t in range(TILES):
        for f in range(FIELDS):
            copy(t, f).wait()


SCALAR = pl.BlockSpec(memory_space=pltpu.SMEM)
LOCAL = pl.BlockSpec(memory_space=pltpu.VMEM)
FAR = pl.BlockSpec(memory_space=pltpu.HBM)


def call(body, operands, specs, outs, out_specs, scratch, cost):
    return pl.pallas_call(
        body,
        out_shape=outs,
        in_specs=specs,
        out_specs=out_specs,
        scratch_shapes=scratch,
        compiler_params=pltpu.CompilerParams(vmem_limit_bytes=VMEM_LIMIT),
        cost_estimate=pl.CostEstimate(flops=cost, bytes_accessed=2_600_000, transcendentals=0),
        name=body.__name__,
    )(*operands)


def exchange(dom_perms, grp_perms, faces):
    x_even, x_odd, y_even, y_odd = faces
    both = ("dom", "grp")
    return (
        lax.ppermute(x_odd, both, dom_perms[1]),
        lax.ppermute(x_even, "dom", dom_perms[0]),
        lax.ppermute(y_odd, "grp", grp_perms[1]),
        lax.ppermute(y_even, "grp", grp_perms[0]),
    )


def pair_swaps(n_dom, n_grp):
    even = lambda n: [(i, i ^ 1) for i in range(n)]
    other = lambda i: ((i - 1) ^ 1) + 1
    dom_odd = []
    for i in range(n_dom):
        for j in range(n_grp):
            if 0 < i < n_dom - 1:
                target = other(i) * n_grp + j
            else:
                target = i * n_grp + (j ^ 1)
            dom_odd.append((i * n_grp + j, target))
    grp_odd = [(j, other(j) if 0 < j < n_grp - 1 else n_grp - 1 - j) for j in range(n_grp)]
    return (even(n_dom), dom_odd), (even(n_grp), grp_odd)


def per_device(n_dom, n_grp, modal, vel, den, snd, g0, g1, g2, orders):
    dom_perms, grp_perms = pair_swaps(n_dom, n_grp)
    swap = functools.partial(exchange, dom_perms, grp_perms)
    shape = modal.shape
    modal = modal.reshape(FIELDS, MODES, MODES * MODES, TILES * LANES)
    small = [vel, den, snd, g2, orders]
    face = jax.ShapeDtypeStruct(FACE, F32)
    bulk = jax.ShapeDtypeStruct(BULK, F32)
    sems = pltpu.SemaphoreType.DMA((TILES, FIELDS))
    plane = (FIELDS, MODES * MODES, LANES)
    q0, coefs, sums, *x_faces = call(
        first_faces,
        tuple(pltpu.with_memory_space_constraint(x, pltpu.HBM) for x in (*small, modal)),
        [FAR] * 6,
        (bulk, jax.ShapeDtypeStruct(COEFS, F32), jax.ShapeDtypeStruct((4,) + FACE, F32)) + (face,) * 2,
        (LOCAL,) * 5,
        [sems]
        + [pltpu.VMEM(x.shape, x.dtype) for x in small]
        + [pltpu.SemaphoreType.DMA((len(small),))],
        2_000_000,
    )
    y_faces = call(first_grp_faces, (coefs, sums), [LOCAL] * 2, (face,) * 2, (LOCAL,) * 2, [], 200_000)
    halos = swap((*x_faces, *y_faces))
    r1, traces = call(
        local_rate,
        (coefs, g0, g1, sums, q0),
        [LOCAL, SCALAR, SCALAR, LOCAL, LOCAL],
        (bulk, jax.ShapeDtypeStruct((4,) + FACE, F32)),
        (LOCAL,) * 2,
        [pltpu.VMEM(BULK, F32)],
        20_000_000_000,
    )
    made = (coefs, g0, g1, traces, *halos)
    specs = [LOCAL, SCALAR, SCALAR] + [LOCAL] * 5
    work = [pltpu.VMEM((4,) + plane, F32)]
    ready = call(
        cross_terms,
        (coefs, g1, traces, *halos[2:]),
        [LOCAL, SCALAR] + [LOCAL] * 3,
        jax.ShapeDtypeStruct((2,) + FACE, F32),
        LOCAL,
        [],
        500_000,
    )
    *x_faces, weights = call(
        second_dom_faces,
        (coefs, g0, ready, *halos[:2]),
        [LOCAL, SCALAR] + [LOCAL] * 3,
        (face, face, jax.ShapeDtypeStruct((TILES, 2, MODES, LANES), F32)),
        (LOCAL,) * 3,
        work,
        1_000_000,
    )
    y_faces = call(
        second_grp_faces, (weights, *made), [LOCAL] + specs, (face,) * 2, (LOCAL,) * 2, work, 1_000_000
    )
    last = swap((*x_faces, *y_faces))
    part = call(
        second_local,
        (coefs, g0, g1, q0, r1, *halos),
        [LOCAL, SCALAR, SCALAR] + [LOCAL] * 6,
        bulk,
        LOCAL,
        [pltpu.VMEM(BULK, F32), pltpu.VMEM(BULK, F32)],
        20_000_000,
    )
    out = call(
        last_add,
        (coefs, g0, g1, part, *last),
        [LOCAL, SCALAR, SCALAR] + [LOCAL] * 5,
        jax.ShapeDtypeStruct(modal.shape, F32),
        FAR,
        [pltpu.VMEM(BULK, F32), sems],
        4_000_000,
    )
    return out.reshape(shape)


def solution(mesh):
    placed = (
        P(None, None, None, None, ("dom", "grp")),
        P(None, ("dom", "grp")),
        P(("dom", "grp")),
        P(("dom", "grp")),
        P("dom"),
        P("grp"),
        P(),
        P(("dom", "grp")),
    )
    return jax.shard_map(
        functools.partial(per_device, mesh.shape["dom"], mesh.shape["grp"]),
        mesh=mesh,
        in_specs=placed,
        out_specs=P(None, None, None, None, ("dom", "grp")),
        check_vma=False,
    )
```

```python
import functools

import jax
import jax.numpy as jnp
from jax import lax
from jax.experimental import pallas as pl
from jax.experimental.pallas import tpu as pltpu
from jax.sharding import PartitionSpec as P

HALF_WAVE = 1.25
TIME_STEP = 0.01
SECTION_A2 = -0.4178904745
SECTION_B1 = 0.1496590219993
SECTION_B2 = 0.3792103129999
MODES = 8
FIELDS = 5
LANES = 128
TILES = 2
FACE = (TILES, FIELDS, MODES * MODES, LANES)
BULK = (TILES, FIELDS, MODES, MODES * MODES, LANES)
F32 = jnp.float32
VMEM_LIMIT = 24 * 1024 * 1024


def rows(m):
    if isinstance(m, int):
        return pl.ds(m * MODES, MODES)
    return pl.ds(pl.multiple_of(m * MODES, MODES), MODES)


def strided(m):
    return pl.ds(m, MODES, stride=MODES)


def flux(q, d, u, rho, inv, stiff):
    n = q[1 + d]
    out = [u * q[0] + rho * n, u * q[1], u * q[2], u * q[3], u * q[4] + stiff * n]
    out[1 + d] = out[1 + d] + inv * q[4]
    return out


FLOW, RHO, INVERSE, STIFF, THIRD, LEVEL, WEIGHT, LIVE = 0, 3, 4, 5, 6, 7, 15, 17
COEFS = (TILES, 25, MODES, LANES)


def spread(ref, t, row=0):
    lanes = pl.ds(t * LANES, LANES)
    part = ref[lanes].reshape(1, -1) if len(ref.shape) == 1 else ref[pl.ds(row, 1), lanes]
    return jnp.broadcast_to(part, (MODES, LANES))


def store_coefs(coefs, vel, den, snd, g2, orders):
    third = lax.broadcasted_iota(jnp.int32, (MODES, LANES), 0)
    for t in range(TILES):
        for k in range(3):
            coefs[t, FLOW + k] = spread(vel, t, k)
        rho, c = spread(den, t), spread(snd, t)
        coefs[t, RHO] = rho
        coefs[t, INVERSE] = 1.0 / rho
        coefs[t, STIFF] = rho * c * c
        coefs[t, THIRD] = spread(g2, t)
        order = jnp.broadcast_to(orders[pl.ds(t, 1)].reshape(1, 1), (MODES, LANES))
        for k in range(MODES):
            coefs[t, LEVEL + k] = jnp.where(jnp.maximum(third, k) <= order, 1.0, 0.0).astype(F32)
            coefs[t, LIVE + k] = jnp.where(order >= k, 1.0, 0.0).astype(F32)
        for parity in range(2):
            coefs[t, WEIGHT + parity] = sum(
                jnp.where(order >= m, m + 0.5, 0.0).astype(F32) for m in range(parity, MODES, 2)
            )


def medium(coefs, t):
    return [coefs[t, FLOW + k] for k in range(3)], coefs[t, RHO], coefs[t, INVERSE], coefs[t, STIFF]


def place():
    out = []
    for axis in ("dom", "grp"):
        i = lax.axis_index(axis)
        n = lax.axis_size(axis)
        sign = (1 - 2 * lax.rem(i, 2)).astype(F32)
        has = jnp.logical_and(i > 0, i < n - 1)
        out.append((sign, has))
    return out


def write_faces(d, sign, coef, sums, slots, t):
    us, rho, inv, stiff = coef
    half = 0.5 * sign
    u = half * us[d]
    near, far = HALF_WAVE + u, HALF_WAVE - u
    rho, inv, stiff = half * rho, half * inv, half * stiff

    for m in range(MODES):
        even = [sums[2 * d, f, rows(m), :] for f in range(FIELDS)]
        odd = [sign * sums[2 * d + 1, f, rows(m), :] for f in range(FIELDS)]
        one = flux([a + b for a, b in zip(even, odd)], d, near, rho, inv, stiff)
        two = flux([a - b for a, b in zip(even, odd)], d, far, -rho, -inv, -stiff)
        for f in range(FIELDS):
            slots[0][t, f, rows(m), :] = one[f]
            slots[1][t, f, rows(m), :] = two[f]


def halo_scales(masks, has, scale):
    other = jnp.where(has, scale, 0.0)
    return [(scale * mask, other * mask) for mask in masks]


def halo_sides(slots, scales, t, f):
    out = []
    for m, (one, two) in enumerate(scales):
        near = one * slots[0][t, f, rows(m), :]
        far = two * slots[1][t, f, rows(m), :]
        out.append([near + far, near - far])
    return out


def first_faces(*refs):
    small, (modal, q0, coefs, sums, x_even, x_odd), (sems, *held, small_sems) = refs[:5], refs[5:11], refs[11:]

    def copy(t, f):
        return pltpu.make_async_copy(modal.at[f, :, :, pl.ds(t * LANES, LANES)], q0.at[t, f], sems.at[t, f])

    for f in range(FIELDS):
        copy(0, f).start()
    loads = [pltpu.make_async_copy(a, b, small_sems.at[i]) for i, (a, b) in enumerate(zip(small, held))]
    for load in loads:
        load.start()
    for f in range(FIELDS):
        copy(1, f).start()
    (sign_x, _), _ = place()
    for load in loads:
        load.wait()
    store_coefs(coefs, *held)

    for t in range(TILES):
        for f in range(FIELDS):
            copy(t, f).wait()
            e0 = [None] * MODES
            o0 = [None] * MODES
            for a in range(MODES):
                e1 = o1 = None
                for b in range(MODES):
                    q = coefs[t, LEVEL + max(a, b)] * q0[t, f, a, rows(b), :]
                    q0[t, f, a, rows(b), :] = q
                    if a % 2 == 0:
                        e0[b] = q if e0[b] is None else e0[b] + q
                    else:
                        o0[b] = q if o0[b] is None else o0[b] + q
                    if b % 2 == 0:
                        e1 = q if e1 is None else e1 + q
                    else:
                        o1 = q if o1 is None else o1 + q
                sums[2, t, f, rows(a), :] = e1
                sums[3, t, f, rows(a), :] = o1
            for b in range(MODES):
                sums[0, t, f, rows(b), :] = e0[b]
                sums[1, t, f, rows(b), :] = o0[b]
        write_faces(0, sign_x, medium(coefs, t), sums.at[:, t], (x_even, x_odd), t)


def first_grp_faces(coefs, sums, y_even, y_odd):
    _, (sign_y, _) = place()
    for t in range(TILES):
        write_faces(1, sign_y, medium(coefs, t), sums.at[:, t], (y_even, y_odd), t)


def scaled(coef, d, s):
    us, rho, inv, stiff = coef
    return s * us[d], s * rho, s * inv, s * stiff


def bases(d, even, odd, us, k):
    a_odd = flux(odd, d, *us)
    a_even = flux(even, d, *us)
    return (
        [-0.5 * (x + k * e) for x, e in zip(a_odd, even)],
        [-0.5 * (x + k * o) for x, o in zip(a_even, odd)],
    )


def parity_sums(load):
    even, odd = load(0), load(1)
    for m in range(2, MODES, 2):
        even = [a + b for a, b in zip(even, load(m))]
        odd = [a + b for a, b in zip(odd, load(m + 1))]
    return even, odd


def sweep(d, load, even, odd, us, emit):
    run = [even, odd]
    for m in range(MODES):
        here = run[m % 2]
        emit(m, [(2.0 * m + 1.0) * a for a in here] if m else here)
        if m < MODES - 1:
            w = flux(load(m), d, *us)
            run[1 - m % 2] = [a + b for a, b in zip(run[1 - m % 2], w)]


def third_direction(q, acc, coefs, metric, h):
    lane = lax.broadcasted_iota(jnp.int32, (MODES, LANES), 1)
    first, last = lane == 0, lane == LANES - 1

    def line(a, carry):
        def loader(t):
            return lambda m: [q[t, f, a, strided(m), :] for f in range(FIELDS)]

        own, up, down = [], [], []
        for t in range(TILES):
            even, odd = parity_sums(loader(t))
            own.append((even, odd))
            us, rho, inv, stiff = medium(coefs, t)
            u = 0.5 * us[2]
            rho, inv, stiff = 0.5 * rho, 0.5 * inv, 0.5 * stiff
            upper = flux([x + y for x, y in zip(even, odd)], 2, HALF_WAVE + u, rho, inv, stiff)
            lower = flux([x - y for x, y in zip(even, odd)], 2, HALF_WAVE - u, -rho, -inv, -stiff)
            up.append([pltpu.roll(x, 1, 1) for x in upper])
            down.append([pltpu.roll(x, LANES - 1, 1) for x in lower])
        for t in range(TILES):
            s = h * coefs[t, THIRD]
            half = 0.5 * s
            us = scaled(medium(coefs, t), 2, s)
            base_e, base_o = bases(2, *own[t], us, 2.0 * HALF_WAVE * s)
            for f in range(FIELDS):
                prior = jnp.where(first, up[1 - t][f], up[t][f])
                after = jnp.where(last, down[1 - t][f], down[t][f])
                base_e[f] = base_e[f] + half * (after + prior)
                base_o[f] = base_o[f] + half * (after - prior)

            def emit(m, terms):
                for f in range(FIELDS):
                    acc[t, f, a, strided(m), :] = terms[f]

            sweep(2, loader(t), base_e, base_o, us, emit)
        return carry

    lax.fori_loop(0, MODES, line, 0, unroll=2)


def second_direction(q, acc, coefs, metric, h):
    for t in range(TILES):
        s = h * metric[1]
        us = scaled(medium(coefs, t), 1, s)

        def line(a, carry):
            def load(m):
                return [q[t, f, a, rows(m), :] for f in range(FIELDS)]

            even, odd = parity_sums(load)
            base_e, base_o = bases(1, even, odd, us, 2.0 * HALF_WAVE * s)

            def emit(m, terms):
                for f in range(FIELDS):
                    acc[t, f, a, rows(m), :] = acc[t, f, a, rows(m), :] + terms[f]

            sweep(1, load, base_e, base_o, us, emit)
            return carry

        lax.fori_loop(0, MODES, line, 0, unroll=2)


def first_direction(q, acc, coefs, metric, h, finish):
    for t in range(TILES):
        s = h * metric[0]
        us = scaled(medium(coefs, t), 0, s)

        def line(b, carry):
            def load(m):
                return [q[t, f, m, rows(b), :] for f in range(FIELDS)]

            even, odd = parity_sums(load)
            base_e, base_o = bases(0, even, odd, us, 2.0 * HALF_WAVE * s)

            kept = {}

            def emit(m, terms):
                finish(t, b, m, [acc[t, f, m, rows(b), :] + terms[f] for f in range(FIELDS)], kept)

            sweep(0, load, base_e, base_o, us, emit)
            return carry

        lax.fori_loop(0, MODES, line, 0, unroll=2)


def local_rate(coefs, g0, g1, sums, q0, r1, traces, acc):
    metric = g0[0], g1[0]
    third_direction(q0, acc, coefs, metric, TIME_STEP)
    second_direction(q0, acc, coefs, metric, TIME_STEP)

    def finish(t, b, a, totals, kept):
        level = coefs[t, LEVEL + jnp.maximum(a, b)]
        for f in range(FIELDS):
            rate = level * totals[f]
            r1[t, f, a, rows(b), :] = rate
            kept[a % 2, f] = rate if a < 2 else kept[a % 2, f] + rate
        if a == MODES - 1:
            for (parity, f), total in kept.items():
                traces[parity, t, f, rows(b), :] = sums[parity, t, f, rows(b), :] + SECTION_B1 * total

    first_direction(q0, acc, coefs, metric, TIME_STEP, finish)
    for t in range(TILES):

        def field(f, carry):
            for a in range(MODES):
                for parity in range(2):
                    total = r1[t, f, a, rows(parity), :]
                    for b in range(parity + 2, MODES, 2):
                        total = total + r1[t, f, a, rows(b), :]
                    traces[2 + parity, t, f, rows(a), :] = sums[2 + parity, t, f, rows(a), :] + SECTION_B1 * total
            return carry

        lax.fori_loop(0, FIELDS, field, 0)


def second_faces(d, coefs, g0, g1, traces, xo, xe, yo, ye, even, odd, sums, table=None):
    (sign_x, has_x), (sign_y, has_y) = place()
    s = SECTION_B1 * TIME_STEP
    sides = (((xe, xo), has_x, s * g0[0]), ((ye, yo), has_y, s * g1[0]))
    signs = (sign_x, sign_y)
    for t in range(TILES):
        mask = [coefs[t, LEVEL + k] for k in range(MODES)]
        live = coefs.at[t, pl.ds(WEIGHT, 2)] if table is None else table.at[t]
        weights = live[0], signs[d] * live[1]
        scales = [halo_scales(mask, has, scale) for _, has, scale in sides]
        heavy = [(m + 0.5) * mask[m] * (signs[1 - d] if m % 2 else 1.0) for m in range(MODES)]
        for f in range(FIELDS):
            along, other = (halo_sides(sides[k][0], scales[k], t, f) for k in (d, 1 - d))
            across = [
                [sum((other[m][kind] for m in range(parity + 2, MODES, 2)), other[parity][kind]) for parity in range(2)]
                for kind in range(2)
            ]
            for m in range(MODES):
                for parity in range(2):
                    sums[2 * d + parity, f, rows(m), :] = traces[2 * d + parity, t, f, rows(m), :] + (
                        weights[parity] * along[m][parity] + heavy[m] * across[m % 2][parity]
                    )
        write_faces(d, signs[d], medium(coefs, t), sums, (even, odd), t)


def second_dom_faces(*refs):
    *refs, weights, sums = refs
    for t in range(TILES):
        weights[t] = refs[0][t, pl.ds(WEIGHT, 2)]
    second_faces(0, *refs, sums)


def second_grp_faces(weights, *refs):
    second_faces(1, *refs, weights)


def halo_terms(coefs, t, sides):
    mask = [coefs[t, LEVEL + k] for k in range(MODES)]
    plain = [(m + 0.5) * coefs[t, LIVE + m] for m in range(MODES)]
    scales = [halo_scales(mask, has, scale) for _, has, scale, _ in sides]
    weights = [[sign * w if m % 2 else w for m, w in enumerate(plain)] for *_, sign in sides]

    def of_field(f):
        first, second = (halo_sides(sides[k][0], scales[k], t, f) for k in range(2))
        return lambda a, b: weights[0][a] * first[b][a % 2] + weights[1][b] * second[a][b % 2]

    return of_field


def second_local(coefs, g0, g1, q0, r1, xo, xe, yo, ye, part, q1, acc):
    metric = g0[0], g1[0]
    (sign_x, has_x), (sign_y, has_y) = place()
    sides = (((xe, xo), has_x, TIME_STEP * metric[0], sign_x), ((ye, yo), has_y, TIME_STEP * metric[1], sign_y))
    for t in range(TILES):
        of_field = halo_terms(coefs, t, sides)

        def field(f, carry):
            term = of_field(f)
            for a in range(MODES):
                for b in range(MODES):
                    rate = r1[t, f, a, rows(b), :] + term(a, b)
                    q = q0[t, f, a, rows(b), :] + SECTION_B1 * rate
                    q1[t, f, a, rows(b), :] = q
                    part[t, f, a, rows(b), :] = q + (SECTION_B2 * SECTION_A2) * rate
            return carry

        lax.fori_loop(0, FIELDS, field, 0)
    third_direction(q1, acc, coefs, metric, SECTION_B2 * TIME_STEP)
    second_direction(q1, acc, coefs, metric, SECTION_B2 * TIME_STEP)

    def finish(t, b, a, totals, kept):
        level = coefs[t, LEVEL + jnp.maximum(a, b)]
        for f in range(FIELDS):
            part[t, f, a, rows(b), :] = part[t, f, a, rows(b), :] + level * totals[f]

    first_direction(q1, acc, coefs, metric, SECTION_B2 * TIME_STEP, finish)


def last_add(coefs, g0, g1, part, xo, xe, yo, ye, out, done, sems):
    (sign_x, has_x), (sign_y, has_y) = place()
    s = SECTION_B2 * TIME_STEP
    sides = (((xe, xo), has_x, s * g0[0], sign_x), ((ye, yo), has_y, s * g1[0], sign_y))

    def copy(t, f):
        lanes = pl.ds(pl.multiple_of(t * LANES, LANES), LANES)
        return pltpu.make_async_copy(done.at[t, f], out.at[f, :, :, lanes], sems.at[t, f])

    def tile(t, carry):
        of_field = halo_terms(coefs, t, sides)

        def field(f, carry):
            term = of_field(f)
            for a in range(MODES):
                for b in range(MODES):
                    done[t, f, a, rows(b), :] = part[t, f, a, rows(b), :] + term(a, b)
            copy(t, f).start()
            return carry

        return lax.fori_loop(0, FIELDS, field, carry)

    lax.fori_loop(0, TILES, tile, 0)
    for t in range(TILES):
        for f in range(FIELDS):
            copy(t, f).wait()


SCALAR = pl.BlockSpec(memory_space=pltpu.SMEM)
LOCAL = pl.BlockSpec(memory_space=pltpu.VMEM)
FAR = pl.BlockSpec(memory_space=pltpu.HBM)


def call(body, operands, specs, outs, out_specs, scratch, cost):
    return pl.pallas_call(
        body,
        out_shape=outs,
        in_specs=specs,
        out_specs=out_specs,
        scratch_shapes=scratch,
        compiler_params=pltpu.CompilerParams(vmem_limit_bytes=VMEM_LIMIT),
        cost_estimate=pl.CostEstimate(flops=cost, bytes_accessed=2_600_000, transcendentals=0),
        name=body.__name__,
    )(*operands)


def exchange(dom_perms, grp_perms, faces):
    x_even, x_odd, y_even, y_odd = faces
    both = ("dom", "grp")
    return (
        lax.ppermute(x_odd, both, dom_perms[1]),
        lax.ppermute(x_even, "dom", dom_perms[0]),
        lax.ppermute(y_odd, both, grp_perms[1]),
        lax.ppermute(y_even, "grp", grp_perms[0]),
    )


def pair_swaps(n_dom, n_grp):
    even = lambda n: [(i, i ^ 1) for i in range(n)]
    other = lambda i: ((i - 1) ^ 1) + 1
    dom_odd = []
    for i in range(n_dom):
        for j in range(n_grp):
            if 0 < i < n_dom - 1:
                target = other(i) * n_grp + j
            else:
                target = i * n_grp + (j ^ 1)
            dom_odd.append((i * n_grp + j, target))
    grp_odd = []
    for i in range(n_dom):
        for j in range(n_grp):
            if 0 < j < n_grp - 1:
                target = i * n_grp + other(j)
            elif i % 4 in (1, 2):
                target = (i ^ 4) * n_grp + j
            else:
                target = i * n_grp + n_grp - 1 - j
            grp_odd.append((i * n_grp + j, target))
    return (even(n_dom), dom_odd), (even(n_grp), grp_odd)


def per_device(n_dom, n_grp, modal, vel, den, snd, g0, g1, g2, orders):
    dom_perms, grp_perms = pair_swaps(n_dom, n_grp)
    swap = functools.partial(exchange, dom_perms, grp_perms)
    shape = modal.shape
    modal = modal.reshape(FIELDS, MODES, MODES * MODES, TILES * LANES)
    small = [vel, den, snd, g2, orders]
    face = jax.ShapeDtypeStruct(FACE, F32)
    bulk = jax.ShapeDtypeStruct(BULK, F32)
    sems = pltpu.SemaphoreType.DMA((TILES, FIELDS))
    plane = (FIELDS, MODES * MODES, LANES)
    q0, coefs, sums, *x_faces = call(
        first_faces,
        tuple(pltpu.with_memory_space_constraint(x, pltpu.HBM) for x in (*small, modal)),
        [FAR] * 6,
        (bulk, jax.ShapeDtypeStruct(COEFS, F32), jax.ShapeDtypeStruct((4,) + FACE, F32)) + (face,) * 2,
        (LOCAL,) * 5,
        [sems]
        + [pltpu.VMEM(x.shape, x.dtype) for x in small]
        + [pltpu.SemaphoreType.DMA((len(small),))],
        2_000_000,
    )
    y_faces = call(first_grp_faces, (coefs, sums), [LOCAL] * 2, (face,) * 2, (LOCAL,) * 2, [], 200_000)
    halos = swap((*x_faces, *y_faces))
    r1, traces = call(
        local_rate,
        (coefs, g0, g1, sums, q0),
        [LOCAL, SCALAR, SCALAR, LOCAL, LOCAL],
        (bulk, jax.ShapeDtypeStruct((4,) + FACE, F32)),
        (LOCAL,) * 2,
        [pltpu.VMEM(BULK, F32)],
        16_000_000,
    )
    made = (coefs, g0, g1, traces, *halos)
    specs = [LOCAL, SCALAR, SCALAR] + [LOCAL] * 5
    work = [pltpu.VMEM((4,) + plane, F32)]
    *x_faces, weights = call(
        second_dom_faces,
        made,
        specs,
        (face, face, jax.ShapeDtypeStruct((TILES, 2, MODES, LANES), F32)),
        (LOCAL,) * 3,
        work,
        1_000_000,
    )
    y_faces = call(
        second_grp_faces, (weights, *made), [LOCAL] + specs, (face,) * 2, (LOCAL,) * 2, work, 1_000_000
    )
    last = swap((*x_faces, *y_faces))
    part = call(
        second_local,
        (coefs, g0, g1, q0, r1, *halos),
        [LOCAL, SCALAR, SCALAR] + [LOCAL] * 6,
        bulk,
        LOCAL,
        [pltpu.VMEM(BULK, F32), pltpu.VMEM(BULK, F32)],
        20_000_000,
    )
    out = call(
        last_add,
        (coefs, g0, g1, part, *last),
        [LOCAL, SCALAR, SCALAR] + [LOCAL] * 5,
        jax.ShapeDtypeStruct(modal.shape, F32),
        FAR,
        [pltpu.VMEM(BULK, F32), sems],
        4_000_000,
    )
    return out.reshape(shape)


def solution(mesh):
    placed = (
        P(None, None, None, None, ("dom", "grp")),
        P(None, ("dom", "grp")),
        P(("dom", "grp")),
        P(("dom", "grp")),
        P("dom"),
        P("grp"),
        P(),
        P(("dom", "grp")),
    )
    return jax.shard_map(
        functools.partial(per_device, mesh.shape["dom"], mesh.shape["grp"]),
        mesh=mesh,
        in_specs=placed,
        out_specs=P(None, None, None, None, ("dom", "grp")),
        check_vma=False,
    )
```
